32 devices in a mesh: dp: 4 (over x, core), fsdp: 8 (over z, y).
Axes of the slice: x: 2, y: 2, z: 4, core: 2. Of those that a mesh axis runs over, the one named last changes fastest.
Arguments:
- xbc: bfloat16 [4096, 10240], P(('dp', 'fsdp')), may hold values from -6 to 6
- zgate: bfloat16 [4096, 8192], P(('dp', 'fsdp')), may hold values from -6 to 6
- dt_raw: float32 [4096, 128], P(('dp', 'fsdp')), may hold values from -5 to 5
- prompt_states: bfloat16 [8, 128, 64, 128], P(None, ('dp', 'fsdp')), may hold values from -3 to 3
- conv_tails: bfloat16 [8, 3, 10240], P(None, None, ('dp', 'fsdp')), may hold values from -6 to 6
- resp_prompt: int32 [128], replicated, may hold values from 0 to 7, as said below
- resp_lengths: int32 [32, 4], P(('dp', 'fsdp')), may hold values from 1 to 80, 128 in all within a row
- rewards: float32 [128], replicated, may hold values from -4 to 4
- upstream: bfloat16 [4096, 8192], P(('dp', 'fsdp')), may hold values from -6 to 6
- conv_weight: float32 [4, 10240], P(None, 'fsdp'), may hold values from -3 to 3
- conv_bias: float32 [10240], P('fsdp'), may hold values from -3 to 3
- dt_bias: float32 [128], P('fsdp'), may hold values from -3 to -1
- a_log: float32 [128], P('fsdp'), may hold values from -5 to -0.7
- d_skip: float32 [128], P('fsdp'), may hold values from 0.5 to 1.5
- norm_gain: float32 [8192], P('fsdp'), may hold values from 0.5 to 1.5
Outputs:
- grad_xbc: bfloat16 [4096, 10240], P(('dp', 'fsdp'))
- grad_zgate: bfloat16 [4096, 8192], P(('dp', 'fsdp'))
- grad_dt_raw: float32 [4096, 128], P(('dp', 'fsdp'))
- grad_prompt_states: float32 [8, 128, 64, 128], P(None, ('dp', 'fsdp'))
- grad_conv_tails: float32 [8, 3, 10240], P(None, None, ('dp', 'fsdp'))
- grad_conv_weight: float32 [4, 10240], P(None, 'fsdp')
- grad_conv_bias: float32 [10240], P('fsdp')
- grad_dt_bias: float32 [128], P('fsdp')
- grad_a_log: float32 [128], P('fsdp')
- grad_d_skip: float32 [128], P('fsdp')
- grad_norm_gain: float32 [8192], P('fsdp')
The draws below stay inside these ranges and needn't reach their ends.
Inputs may be any that keep to these rules, and one draw needn't show every extreme that they name: `resp_prompt`: each of the 8 prompts is named by exactly 16 responses. `resp_lengths`: the 4 lengths of one device sum to 128.
All inputs are finite; a program needn't handle non-finite values.
Results may differ from the reference program's by a relative error of at most 0.0011.
Values may be sent and summed in bfloat16 or wider, within the bound.
A program may use at most 192 MiB of HBM per device.

```python
import math
import jax
import jax.numpy as jnp
import numpy as np
from jax import lax

TOK_DEV = 128
DOCS_DEV = 4
GROUP = 16
H = 128
P_SIZE = 64
N = 128
G = 8
GS = 2048
DI = 8192
CONV = 10240
LMAX = 80
HOLDERS = 32
TOKENS = 4096
RESPONSES = 128
PROMPTS = 8
N_DP = 4
N_FSDP = 8


def draw_resp_prompt(key, part):
    key = jax.random.fold_in(key, 7)
    return (jax.random.permutation(key, RESPONSES) // GROUP).astype(jnp.int32)


def shard_levels(own_key, dims, pieces, least, largest):
    level, own = 1.0, jax.random.fold_in(own_key, 6)
    for dim, blocks in pieces:
        heights = jnp.exp(jax.random.uniform(jax.random.fold_in(own, dim), (blocks,), jnp.float32, least / len(pieces), largest / len(pieces)))
        level = level * jnp.repeat(heights, dims[dim] // blocks).reshape([-1 if axis == dim else 1 for axis in range(len(dims))])
    return level


def split_up(count, total, most, slope):
    loads = [(1 << 20) // math.isqrt(grade ** slope) + 1 for grade in range(2, count + 1)]
    spare, given = total - most - (count - 1), [1] * (count - 1)
    while spare > 0:
        free = [i for i in range(count - 1) if given[i] < most]
        whole, left = sum([loads[i] for i in free]), spare
        for i in free:
            more = min(most - given[i], max(1, left * loads[i] // whole), spare)
            given[i] = given[i] + more
            spare = spare - more
    return np.array([most] + given)


def uneven(rng, count, total, reach, slope):
    if count == 2:
        one = jax.random.randint(rng, (), max(1, total - reach), min(reach, total - 1) + 1)
        return jnp.stack([one, total - one])
    tallies = jnp.asarray(split_up(count, total, reach, slope), jnp.int32)
    couples = (count - 1) // 2
    donor, taker = tallies[1:1 + 2 * couples:2], tallies[2:2 + 2 * couples:2]
    room = jnp.minimum(donor - 1, reach - taker)
    passed = jax.random.randint(jax.random.fold_in(rng, 1), (couples,), 0, 1 << 20) % (room + 1)
    tallies = tallies.at[1:1 + 2 * couples:2].set(donor - passed).at[2:2 + 2 * couples:2].set(taker + passed)
    return tallies[jax.random.permutation(jax.random.fold_in(rng, 2), count)]


def bell_draw(key, dims, width, most, shards=(), kind=jnp.bfloat16):
    factor_of = shard_levels(key, dims, shards, -0.22, 0.18) if shards else 1.0
    result = jax.random.normal(key, dims, jnp.float32) * width * factor_of
    return jnp.minimum(jnp.maximum(result, -most), most).astype(kind)


def setup_inputs(seed: int = 0) -> dict:
    key_of = jax.random.split(jax.random.key(seed), 16)
    xbc = bell_draw(key_of[0], (TOKENS, CONV), 1.0, 6.0, ((0, 32),))
    zgate = bell_draw(key_of[1], (TOKENS, DI), 1.0, 6.0, ((0, 32),))
    dt_raw = bell_draw(key_of[2], (TOKENS, H), 1.0, 5.0, ((0, 32),), jnp.float32)
    prompt_states = bell_draw(key_of[3], (PROMPTS, H, P_SIZE, N), 0.5, 3.0, ((1, 32),))
    conv_tails = bell_draw(key_of[4], (PROMPTS, 3, CONV), 1.0, 6.0, ((2, 32),))
    resp_prompt = draw_resp_prompt(jax.random.fold_in(key_of[15], 71), 0)
    resp_lengths = jax.vmap(lambda own: uneven(own, DOCS_DEV, TOK_DEV, LMAX, 2))(jax.random.split(key_of[6], HOLDERS)).reshape((HOLDERS, DOCS_DEV)).astype(jnp.int32)
    rewards = bell_draw(key_of[7], (RESPONSES,), 1.0, 4.0, (), jnp.float32)
    upstream = bell_draw(key_of[8], (TOKENS, DI), 1.0, 6.0, ((0, 32),))
    conv_weight = bell_draw(key_of[9], (4, CONV), 4 ** -0.5, 3.0, ((1, 8),), jnp.float32)
    conv_bias = bell_draw(key_of[10], (CONV,), 0.5, 3.0, ((0, 8),), jnp.float32)
    dt_bias = jnp.clip(-3.0 + 2.0 * jax.random.uniform(key_of[11], (H,), jnp.float32) ** shard_levels(key_of[11], (H,), ((0, 8),), -0.2, 0.2), -3.0, -1.0)
    a_log = jnp.clip(-5.0 + 4.3 * jax.random.uniform(key_of[12], (H,), jnp.float32) ** shard_levels(key_of[12], (H,), ((0, 8),), -0.2, 0.2), -5.0, -0.7)
    d_skip = jnp.clip(0.5 + 1.0 * jax.random.uniform(key_of[13], (H,), jnp.float32) ** shard_levels(key_of[13], (H,), ((0, 8),), -0.2, 0.2), 0.5, 1.5)
    norm_gain = jnp.clip(1.0 + 0.1 * jax.random.normal(key_of[14], (DI,), jnp.float32), 0.5, 1.5)
    return {"xbc": xbc, "zgate": zgate, "dt_raw": dt_raw, "prompt_states": prompt_states, "conv_tails": conv_tails, "resp_prompt": resp_prompt, "resp_lengths": resp_lengths, "rewards": rewards, "upstream": upstream, "conv_weight": conv_weight, "conv_bias": conv_bias, "dt_bias": dt_bias, "a_log": a_log, "d_skip": d_skip, "norm_gain": norm_gain}


def advantages(rewards, resp_prompt, prompt_count):
    member = (resp_prompt[:, None] == jnp.arange(prompt_count, dtype=jnp.int32)[None, :]).astype(jnp.float32)
    group_mean = jnp.dot(rewards, member, precision=lax.Precision.HIGHEST) / GROUP
    centred = rewards - jnp.dot(member, group_mean, precision=lax.Precision.HIGHEST)
    spread = jnp.sqrt(jnp.dot(centred * centred, member, precision=lax.Precision.HIGHEST) / GROUP)
    return centred / jnp.dot(member, jnp.maximum(spread, 0.8), precision=lax.Precision.HIGHEST)

def token_layout(lengths, row_count):
    places = jnp.arange(row_count, dtype=jnp.int32)
    doc_ends = jnp.cumsum(lengths).astype(jnp.int32)
    doc_starts = (doc_ends - lengths).astype(jnp.int32)
    member = (places[:, None] >= doc_starts[None, :]) & (places[:, None] < doc_ends[None, :])
    start_tok = lax.optimization_barrier(jnp.sum(jnp.where(member, doc_starts[None, :], 0), axis=1)).astype(jnp.int32)
    return (member, start_tok, (places - start_tok).astype(jnp.int32))

def conv_branch(signal, tail_rows, conv_w, conv_b, member, offset):
    row_count = signal.shape[0]
    summed = conv_w[3][None, :] * signal
    for delay_step in (1, 2, 3):
        lagged = jnp.concatenate([jnp.zeros((delay_step, signal.shape[1]), jnp.float32), signal[:-delay_step]], axis=0)
        summed = summed + jnp.where((offset >= delay_step)[:, None], lagged, 0.0) * conv_w[3 - delay_step][None, :]
    tail_a = tail_rows[:, 0, :]
    tail_b = tail_rows[:, 1, :]
    tail_c = tail_rows[:, 2, :]
    w_zero = conv_w[0][None, :]
    w_one = conv_w[1][None, :]
    w_two = conv_w[2][None, :]
    lead_in = jnp.stack([w_two * tail_c + w_one * tail_b + w_zero * tail_a, w_one * tail_c + w_zero * tail_b, w_zero * tail_c], axis=1)
    select = (member[:, :, None] & (offset[:, None, None] == jnp.arange(3, dtype=jnp.int32)[None, None, :])).astype(jnp.float32)
    summed = summed + jnp.dot(select.reshape(row_count, -1), lead_in.reshape(-1, signal.shape[1]), precision=lax.Precision.HIGHEST)
    return jax.nn.silu(summed + conv_b[None, :])

def mixer_forward(signal, gate_in, dt_in, states, tail_rows, params, member, start_tok, offset):
    conv_w, conv_b, bias_dt, log_rate, skip_all, gain = params
    row_count = signal.shape[0]
    doc_count = states.shape[0]
    inner = H * P_SIZE
    per_group = H // G
    conv_out = conv_branch(signal, tail_rows, conv_w, conv_b, member, offset)
    x_heads = conv_out[:, :inner].reshape(row_count, G, per_group, P_SIZE).transpose(1, 0, 2, 3)
    b_all = conv_out[:, inner:inner + G * N].reshape(row_count, G, N).transpose(1, 0, 2)
    c_all = conv_out[:, inner + G * N:].reshape(row_count, G, N).transpose(1, 0, 2)
    step_size = jax.nn.softplus(dt_in + bias_dt[None, :])
    decay_log = -step_size * jnp.exp(log_rate)[None, :]
    cum_log = jnp.cumsum(decay_log, axis=0)
    base_log = jnp.take(cum_log - decay_log, start_tok, axis=0)
    rel_log = cum_log - base_log
    places = jnp.arange(row_count, dtype=jnp.int32)
    causal = (start_tok[:, None] == start_tok[None, :]) & (places[:, None] >= places[None, :])
    member_f = member.astype(jnp.float32)

    def by_group(table):
        return table.reshape(row_count, G, per_group).transpose(1, 0, 2)
    start_all = states.reshape(doc_count, G, per_group, P_SIZE, N).transpose(1, 0, 2, 3, 4)

    def group_mix(items):
        c_rows, b_rows, x_rows, steps_g, cum_g, rel_g, start_state, skip_gain = items
        scores = jnp.dot(c_rows, b_rows.T, precision=lax.Precision.HIGHEST)
        log_gaps = cum_g.T[:, :, None] - cum_g.T[:, None, :]
        decays = jnp.exp(jnp.where(causal[None], log_gaps, -jnp.inf))
        weights = decays * scores[None] * steps_g.T[:, None, :]
        within = jnp.einsum('kts,skp->tkp', weights, x_rows, precision=lax.Precision.HIGHEST)
        c_masked = member_f[:, :, None] * c_rows[:, None, :]
        carried = jnp.einsum('tdn,dkpn->tkp', c_masked, start_state, precision=lax.Precision.HIGHEST)
        carried = carried * jnp.exp(rel_g)[:, :, None]
        return within + carried + skip_gain[None, :, None] * x_rows
    mixed_out = lax.map(jax.checkpoint(group_mix), (c_all, b_all, x_heads, by_group(step_size), by_group(cum_log), by_group(rel_log), start_all, skip_all.reshape(G, per_group)))
    mixed_out = mixed_out.transpose(1, 0, 2, 3).reshape(row_count, inner)
    gated_out = mixed_out * jax.nn.silu(gate_in)
    grouped = gated_out.reshape(row_count, inner // GS, GS)
    inv_rms = lax.rsqrt(lax.optimization_barrier(jnp.mean(grouped * grouped, axis=-1, keepdims=True)) + 1e-05)
    return (grouped * inv_rms).reshape(row_count, inner) * gain[None, :]

def local_grads(signal_in, gate_in, dt_in, states, tail_rows, params, lengths, upstream, doc_weight):
    member, start_tok, offset = token_layout(lengths, signal_in.shape[0])
    tok_weight = lax.optimization_barrier(jnp.sum(jnp.where(member, doc_weight[None, :], 0.0), axis=1))

    def forward(signal, gate_vals, dt_vals, state_vals, tail_vals, weight_vals):
        return mixer_forward(signal, gate_vals, dt_vals, state_vals, tail_vals, weight_vals, member, start_tok, offset)
    primal_out, pullback = jax.vjp(forward, signal_in.astype(jnp.float32), gate_in.astype(jnp.float32), dt_in, states.astype(jnp.float32), tail_rows.astype(jnp.float32), params)
    return pullback(upstream.astype(jnp.float32) * tok_weight[:, None])

def reference(xbc, zgate, dt_raw, prompt_states, conv_tails, resp_prompt, resp_lengths, rewards, upstream, conv_weight, conv_bias, dt_bias, a_log, d_skip, norm_gain):
    params = (conv_weight, conv_bias, dt_bias, a_log, d_skip, norm_gain)
    advantage = advantages(rewards, resp_prompt, PROMPTS)

    def device_step(running, holder):
        first_row = (holder * TOK_DEV).astype(jnp.int32)
        first_doc = (holder * DOCS_DEV).astype(jnp.int32)
        prompt_ids = lax.dynamic_slice_in_dim(resp_prompt, first_doc, DOCS_DEV)
        lengths = resp_lengths[holder]
        doc_weight = lax.dynamic_slice_in_dim(advantage, first_doc, DOCS_DEV) * (TOK_DEV / (DOCS_DEV * lengths.astype(jnp.float32)))
        gradients = local_grads(lax.dynamic_slice_in_dim(xbc, first_row, TOK_DEV), lax.dynamic_slice_in_dim(zgate, first_row, TOK_DEV), lax.dynamic_slice_in_dim(dt_raw, first_row, TOK_DEV), prompt_states[prompt_ids], conv_tails[prompt_ids], params, lengths, lax.dynamic_slice_in_dim(upstream, first_row, TOK_DEV), doc_weight)
        grad_x, grad_z, grad_dt, grad_state, grad_tail, grad_param = gradients
        state_sum, tail_sum, param_sum = running
        state_sum = state_sum.at[prompt_ids].add(grad_state)
        tail_sum = tail_sum.at[prompt_ids].add(grad_tail)
        param_sum = jax.tree.map(jnp.add, param_sum, grad_param)
        return ((state_sum, tail_sum, param_sum), (grad_x.astype(jnp.bfloat16), grad_z.astype(jnp.bfloat16), grad_dt))
    param_zero = tuple((jnp.zeros(weight.shape, jnp.float32) for weight in params))
    start_carry = (jnp.zeros(prompt_states.shape, jnp.float32), jnp.zeros(conv_tails.shape, jnp.float32), param_zero)
    final_carry, stacked = lax.scan(device_step, start_carry, jnp.arange(N_DP * N_FSDP, dtype=jnp.int32))
    state_sum, tail_sum, param_sum = final_carry
    grad_x, grad_z, grad_dt = stacked
    return (grad_x.reshape(TOKENS, CONV), grad_z.reshape(TOKENS, DI), grad_dt.reshape(TOKENS, H), state_sum, tail_sum, param_sum[0], param_sum[1], param_sum[2], param_sum[3], param_sum[4], param_sum[5])
```

```python
import functools

import jax
import jax.numpy as jnp
from jax import lax
from jax.experimental import pallas as pl
from jax.experimental.pallas import tpu as pltpu
from jax.sharding import PartitionSpec as P

GROUP = 16
H = 128
P_SIZE = 64
N = 128
G = 8
GS = 2048
DI = H * P_SIZE
GN = G * N

CH = 256
HC = CH // P_SIZE
F32 = jnp.float32
BF16 = jnp.bfloat16
NN = (((1,), (0,)), ((), ()))
NT = (((1,), (1,)), ((), ()))


def advantages(rewards, resp_prompt, prompt_count):
    member = (resp_prompt[:, None] == jnp.arange(prompt_count, dtype=jnp.int32)[None, :]).astype(
        jnp.float32
    )
    group_mean = jnp.dot(rewards, member, precision=lax.Precision.HIGHEST) / GROUP
    centred = rewards - jnp.dot(member, group_mean, precision=lax.Precision.HIGHEST)
    spread = jnp.sqrt(jnp.dot(centred * centred, member, precision=lax.Precision.HIGHEST) / GROUP)
    return centred / jnp.dot(member, jnp.maximum(spread, 0.8), precision=lax.Precision.HIGHEST)


def dot(a, b, dims=NN):
    return lax.dot_general(a, b, dims, preferred_element_type=F32)


def split2(a):
    hi = a.astype(BF16)
    return hi, (a - hi.astype(F32)).astype(BF16)


def split3(a):
    hi = a.astype(BF16)
    rest = a - hi.astype(F32)
    mid = rest.astype(BF16)
    return hi, mid, (rest - mid.astype(F32)).astype(BF16)


def dot3(a, b, dims=NN):
    ah, al = split2(a)
    bh, bl = split2(b)
    return dot(ah, bh, dims) + dot(ah, bl, dims) + dot(al, bh, dims)


def exact_left(mask, table):
    hi, mid, lo = split3(table)
    return dot(mask, hi) + dot(mask, mid) + dot(mask, lo)


def colsum(a):
    return jnp.sum(a, axis=0, keepdims=True)


def mixer_kernel(
    dims,
    prompt_ref,
    adv_ref,
    recv_ref,
    tails_ref,
    wv_ref,
    hv_ref,
    states_ref,
    out_ref,
    dstate_ref,
    dtail_ref,
    wg_ref,
    st,
    acc,
    uext,
    co,
    dco,
    ybuf,
    sc,
    sct,
    cmh,
    cml,
    relt,
    rel3,
    se3,
    dred,
    dsc,
    dcc,
    sems,
    out_sem,
):
    rows, docs, chans, inner, heads, groups, fcount, share_rows = dims
    nf = CH // share_rows
    k = pl.program_id(0)
    inner_chunks = inner // CH
    all_chunks = chans // CH
    zoff, upoff, moff = chans, chans + inner, chans + 2 * inner
    b_off, c_off = inner, inner + groups * N

    copies = [
        pltpu.make_async_copy(states_ref.at[:, prompt_ref[k * docs + d]], st.at[d], sems.at[d])
        for d in range(docs)
    ]
    for copy in copies:
        copy.start()

    @pl.when(k == 0)
    def _():
        wg_ref[...] = jnp.zeros_like(wg_ref)
        uext[...] = jnp.zeros_like(uext)

        def clear(f, carry):
            acc[f] = jnp.zeros(acc.shape[1:], F32)
            return carry

        lax.fori_loop(0, fcount, clear, 0)

    meta = recv_ref[0, :, moff : moff + 128].astype(F32)
    lens = [meta[0:1, 96 + d : 97 + d] for d in range(docs)]
    tcol = lax.broadcasted_iota(jnp.int32, (rows, 1), 0).astype(F32)
    trow = lax.broadcasted_iota(jnp.int32, (1, rows), 1).astype(F32)
    doc_col, doc_row = jnp.zeros_like(tcol), jnp.zeros_like(trow)
    start_col, start_row = jnp.zeros_like(tcol), jnp.zeros_like(trow)
    begin = jnp.zeros((1, 1), F32)
    for d in range(docs - 1):
        begin = begin + lens[d]
        doc_col = doc_col + jnp.where(tcol >= begin, 1.0, 0.0)
        doc_row = doc_row + jnp.where(trow >= begin, 1.0, 0.0)
        start_col = jnp.where(tcol >= begin, begin, start_col)
        start_row = jnp.where(trow >= begin, begin, start_row)
    off_col, off_row = tcol - start_col, trow - start_row
    wtok = jnp.zeros_like(tcol)
    for d in range(docs):
        wtok = wtok + jnp.where(
            doc_col == d, adv_ref[k * docs + d] * (rows / (docs * lens[d])), 0.0
        )
    same = doc_col == doc_row
    causal = same & (tcol >= trow)
    causal_t = same & (trow >= tcol)

    ext_row = lax.broadcasted_iota(jnp.int32, (1, 2 * rows), 1).astype(F32)
    ext_col = lax.broadcasted_iota(jnp.int32, (rows + 16, 1), 0).astype(F32)
    shift, shift_t = [], []
    for j in (1, 2, 3):
        src_col = jnp.where(off_col >= j, tcol - j, rows + doc_col * 4 + (3 - j) + off_col)
        src_row = jnp.where(off_row >= j, trow - j, rows + doc_row * 4 + (3 - j) + off_row)
        shift.append(jnp.where(src_col == ext_row, 1.0, 0.0).astype(BF16))
        shift_t.append(jnp.where(src_row == ext_col, 1.0, 0.0).astype(BF16))
    shift = jnp.concatenate(shift, axis=0)
    shift_t = jnp.concatenate(shift_t, axis=1)

    uext[0:rows, :] = recv_ref[0, :, 0:chans]
    uext[rows : rows + 16, :] = tails_ref[0]

    def conv(cs):
        u = uext[:, pl.ds(cs, CH)]
        lag = dot(shift, u)
        taps = [u[0:rows].astype(F32)] + [lag[i * rows : (i + 1) * rows] for i in range(3)]
        w = [wv_ref[3 - j : 4 - j, pl.ds(cs, CH)] for j in range(4)]
        pre = wv_ref[4:5, pl.ds(cs, CH)] + sum(w[j] * taps[j] for j in range(4))
        return pre, taps, w

    def conv_step(i, carry):
        cs = pl.multiple_of(i * CH, CH)
        pre, _, _ = conv(cs)
        co[:, pl.ds(cs, CH)] = pre * jax.nn.sigmoid(pre)
        return carry

    lax.fori_loop(0, all_chunks, conv_step, 0)

    for g in range(groups):
        bg = co[:, b_off + g * N : b_off + (g + 1) * N]
        cg = co[:, c_off + g * N : c_off + (g + 1) * N]
        sc[g] = dot3(cg, bg, NT)
        sct[g] = dot3(bg, cg, NT)
        hi, lo = split2(cg)
        zero = jnp.zeros_like(hi)
        for d in range(docs):
            cmh[g, :, d * N : (d + 1) * N] = jnp.where(doc_col == d, hi, zero)
            cml[g, :, d * N : (d + 1) * N] = jnp.where(doc_col == d, lo, zero)
        dsc[g] = jnp.zeros((rows, rows), F32)
        dcc[g] = jnp.zeros((rows, N), F32)
    dred[...] = jnp.zeros_like(dred)

    dt_pre = meta[:, 0:32] + meta[:, 32:64] + meta[:, 64:96] + hv_ref[0:1, :]
    tail_exp = jnp.exp(-jnp.abs(dt_pre))
    step = jnp.maximum(dt_pre, 0.0) + jnp.log1p(tail_exp)
    rate = -jnp.exp(hv_ref[1:2, :])
    dec = step * rate
    rel = exact_left(jnp.where(causal, 1.0, 0.0).astype(BF16), dec)
    relt[...] = rel.T
    rel3[...] = jnp.concatenate(split3(rel), axis=1)
    se3[0:rows, :] = jnp.concatenate(split3(step), axis=1)
    se3[rows : 2 * rows, :] = jnp.concatenate(split3(jnp.exp(rel)), axis=1)

    def head_onehot(c, width):
        r = lax.broadcasted_iota(jnp.int32, (3 * heads, HC * width), 0)
        r = jnp.where(r >= 2 * heads, r - 2 * heads, jnp.where(r >= heads, r - heads, r))
        lane = lax.broadcasted_iota(jnp.int32, (3 * heads, HC * width), 1)
        return jnp.where(r == c * HC + lane // width, 1.0, 0.0).astype(BF16)

    lane_head = lax.broadcasted_iota(jnp.int32, (1, CH), 1) // P_SIZE

    def block_diag(a):
        zero = jnp.zeros_like(a)
        return jnp.concatenate([jnp.where(lane_head == h, a, zero) for h in range(HC)], axis=0)

    def chunk_tables(c):
        expand = dot(se3[...], head_onehot(c, P_SIZE))
        colb = dot(rel3[...], head_onehot(c, rows))
        rowb = [relt[pl.ds(c * HC + h, 1), :] for h in range(HC)]
        return expand[0:rows], expand[rows : 2 * rows], colb, rowb

    def state_of(d, c):
        return st[d, pl.ds(c * nf, nf)].reshape(CH, N)

    for copy in copies:
        copy.wait()

    def forward_step(c, carry):
        s1, s2 = carry
        cs = pl.multiple_of(c * CH, CH)
        g = c // (inner_chunks // groups)
        stepx, ex, colb, rowb = chunk_tables(c)
        x = co[:, pl.ds(cs, CH)]
        xh, xl = split2(x * stepx)
        score = sc[g]
        w = jnp.concatenate(
            [
                jnp.exp(jnp.where(causal, colb[:, h * rows : (h + 1) * rows] - rowb[h], -1e30))
                * score
                for h in range(HC)
            ],
            axis=1,
        )
        wh, wl = split2(w)
        bh, bl = block_diag(xh), block_diag(xl)
        within = dot(wh, bh) + dot(wh, bl) + dot(wl, bh)
        carried = jnp.zeros((rows, CH), F32)
        for d in range(docs):
            state = state_of(d, c)
            carried = carried + dot(cmh[g, :, d * N : (d + 1) * N], state, NT)
            carried = carried + dot(cml[g, :, d * N : (d + 1) * N], state, NT)
        y = within + ex * carried + wv_ref[6:7, pl.ds(cs, CH)] * x
        ybuf[:, pl.ds(cs, CH)] = y
        z = recv_ref[0, :, pl.ds(zoff + cs, CH)].astype(F32)
        up = recv_ref[0, :, pl.ds(upoff + cs, CH)].astype(F32)
        v = y * (z * jax.nn.sigmoid(z))
        p1 = v * v
        p2 = up * wv_ref[5:6, pl.ds(cs, CH)] * v
        return s1 + p1[:, :128] + p1[:, 128:], s2 + p2[:, :128] + p2[:, 128:]

    zeros = jnp.zeros((rows, 128), F32)
    s1, s2 = lax.fori_loop(0, inner_chunks, forward_step, (zeros, zeros))
    inv = lax.rsqrt(jnp.sum(s1, axis=1, keepdims=True) / GS + 1e-05)
    mean2 = jnp.sum(s2, axis=1, keepdims=True) * wtok / GS
    coef = inv * inv * inv * mean2

    def backward_step(c, carry):
        cs = pl.multiple_of(c * CH, CH)
        g = c // (inner_chunks // groups)
        stepx, ex, colb, rowb = chunk_tables(c)
        x = co[:, pl.ds(cs, CH)]
        y = ybuf[:, pl.ds(cs, CH)]
        z = recv_ref[0, :, pl.ds(zoff + cs, CH)].astype(F32)
        up = recv_ref[0, :, pl.ds(upoff + cs, CH)].astype(F32)
        skip = wv_ref[6:7, pl.ds(cs, CH)]
        sg = jax.nn.sigmoid(z)
        sz = z * sg
        v = y * sz
        dn = up * (wtok * inv)
        wg_ref[5:6, pl.ds(cs, CH)] += colsum(dn * v)
        dv = dn * wv_ref[5:6, pl.ds(cs, CH)] - v * coef
        dy = dv * sz
        out_ref[0, :, pl.ds(chans + cs, CH)] = (dv * y * (sg * (1.0 + z * (1.0 - sg)))).astype(
            BF16
        )
        xs = x * stepx
        xh, xl = split2(xs)
        dyh, dyl = split2(dy)
        bh, bl = block_diag(xh), block_diag(xl)
        dm = dot(dyh, bh, NT) + dot(dyh, bl, NT) + dot(dyl, bh, NT)
        score_t = sct[g]
        total = dsc[g]
        wt = []
        for h in range(HC):
            gap = colb[:, h * rows : (h + 1) * rows] - rowb[h]
            total = total + jnp.exp(jnp.where(causal, gap, -1e30)) * dm[:, h * rows : (h + 1) * rows]
            wt.append(jnp.exp(jnp.where(causal_t, -gap, -1e30)) * score_t)
        dsc[g] = total
        wh, wl = split2(jnp.concatenate(wt, axis=1))
        dh, dl = block_diag(dyh), block_diag(dyl)
        dxs = dot(wh, dh) + dot(wh, dl) + dot(wl, dh)
        dco[:, pl.ds(cs, CH)] = stepx * dxs + skip * dy
        wg_ref[6:7, pl.ds(cs, CH)] += colsum(dy * x)
        both = jnp.concatenate([dy * (y - skip * x) - xs * dxs, dxs * x], axis=0)
        pick = jnp.where(
            lax.broadcasted_iota(jnp.int32, (CH, heads), 0) // P_SIZE + c * HC
            == lax.broadcasted_iota(jnp.int32, (CH, heads), 1),
            1.0,
            0.0,
        ).astype(BF16)
        b1, b2, b3 = split3(both)
        dred[...] += dot(b1, pick) + dot(b2, pick) + dot(b3, pick)
        q = ex * dy
        qh, ql = split2(q)
        qth, qtl = split2(q.T)
        ch, cl = cmh[g], cml[g]
        ds_all = dot(qth, ch) + dot(qtl, ch) + dot(qth, cl)
        back = jnp.zeros((rows, N), F32)
        for d in range(docs):
            p = prompt_ref[k * docs + d]
            acc[pl.ds(c * nf, nf), p] += ds_all[:, d * N : (d + 1) * N].reshape(nf, share_rows, N)
            state = state_of(d, c)
            back = back + jnp.where(doc_col == d, dot(qh, state) + dot(ql, state), 0.0)
        dcc[g] += back
        return carry

    lax.fori_loop(0, inner_chunks, backward_step, 0)

    @pl.when(k == pl.num_programs(0) - 1)
    def _():
        pltpu.make_async_copy(acc, dstate_ref, out_sem).start()

    for g in range(groups):
        bg = co[:, b_off + g * N : b_off + (g + 1) * N]
        cg = co[:, c_off + g * N : c_off + (g + 1) * N]
        dco[:, c_off + g * N : c_off + (g + 1) * N] = dot3(dsc[g], bg) + dcc[g]
        dco[:, b_off + g * N : b_off + (g + 1) * N] = dot3(dsc[g].T, cg)

    ddec = exact_left(jnp.where(causal_t, 1.0, 0.0).astype(BF16), dred[0:rows])
    ddt = (dred[rows : 2 * rows] + ddec * rate) * jax.nn.sigmoid(dt_pre)
    wg_ref[7:8, 0:heads] += colsum(ddt)
    wg_ref[8:9, 0:heads] += colsum(ddec * dec)
    out_ref[0, :, chans + inner :] = jnp.concatenate(
        list(split3(ddt)) + [jnp.zeros((rows, 128 - 3 * heads), BF16)], axis=1
    )

    def conv_back(i, carry):
        cs = pl.multiple_of(i * CH, CH)
        pre, taps, w = conv(cs)
        sg = jax.nn.sigmoid(pre)
        dpre = dco[:, pl.ds(cs, CH)] * (sg * (1.0 + pre * (1.0 - sg)))
        for j in range(4):
            wg_ref[3 - j : 4 - j, pl.ds(cs, CH)] += colsum(dpre * taps[j])
        wg_ref[4:5, pl.ds(cs, CH)] += colsum(dpre)
        hi, lo = split2(jnp.concatenate([w[j] * dpre for j in (1, 2, 3)], axis=0))
        du = dot(shift_t, hi) + dot(shift_t, lo)
        out_ref[0, :, pl.ds(cs, CH)] = (w[0] * dpre + du[0:rows]).astype(BF16)
        dtail_ref[0, :, pl.ds(cs, CH)] = du[rows : rows + 16]
        return carry

    lax.fori_loop(0, all_chunks, conv_back, 0)

    @pl.when(k == pl.num_programs(0) - 1)
    def _():
        pltpu.make_async_copy(acc, dstate_ref, out_sem).wait()


def run_mixer(prompts, adv, recv, tails, wv, hv, states, docs):
    blocks, rows, width = recv.shape
    chans = wv.shape[1]
    fcount, prompt_count, share_rows, _ = states.shape
    inner = fcount * share_rows
    heads = inner // P_SIZE
    groups = (chans - inner) // (2 * N)
    dims = (rows, docs, chans, inner, heads, groups, fcount, share_rows)
    out_width = chans + inner + 128
    smem = pl.BlockSpec(memory_space=pltpu.SMEM)
    hbm = pl.BlockSpec(memory_space=pl.ANY)
    return pl.pallas_call(
        functools.partial(mixer_kernel, dims),
        grid=(blocks,),
        in_specs=[
            smem,
            smem,
            pl.BlockSpec((1, rows, width), lambda i: (i, 0, 0)),
            pl.BlockSpec((1, 16, chans), lambda i: (i, 0, 0)),
            pl.BlockSpec(wv.shape, lambda i: (0, 0)),
            pl.BlockSpec(hv.shape, lambda i: (0, 0)),
            hbm,
        ],
        out_specs=[
            pl.BlockSpec((1, rows, out_width), lambda i: (i, 0, 0)),
            hbm,
            pl.BlockSpec((1, 16, chans), lambda i: (i, 0, 0)),
            pl.BlockSpec((16, chans), lambda i: (0, 0)),
        ],
        out_shape=[
            jax.ShapeDtypeStruct((blocks, rows, out_width), BF16),
            jax.ShapeDtypeStruct(states.shape, F32),
            jax.ShapeDtypeStruct((blocks, 16, chans), F32),
            jax.ShapeDtypeStruct((16, chans), F32),
        ],
        scratch_shapes=[
            pltpu.VMEM((docs, fcount, share_rows, N), BF16),
            pltpu.VMEM(states.shape, F32),
            pltpu.VMEM((2 * rows, chans), BF16),
            pltpu.VMEM((rows, chans), F32),
            pltpu.VMEM((rows, chans), F32),
            pltpu.VMEM((rows, inner), F32),
            pltpu.VMEM((groups, rows, rows), F32),
            pltpu.VMEM((groups, rows, rows), F32),
            pltpu.VMEM((groups, rows, docs * N), BF16),
            pltpu.VMEM((groups, rows, docs * N), BF16),
            pltpu.VMEM((heads, rows), F32),
            pltpu.VMEM((rows, 3 * heads), BF16),
            pltpu.VMEM((2 * rows, 3 * heads), BF16),
            pltpu.VMEM((2 * rows, heads), F32),
            pltpu.VMEM((groups, rows, rows), F32),
            pltpu.VMEM((groups, rows, N), F32),
            pltpu.SemaphoreType.DMA((docs,)),
            pltpu.SemaphoreType.DMA,
        ],
        compiler_params=pltpu.CompilerParams(
            dimension_semantics=("arbitrary",), vmem_limit_bytes=60 * 1024 * 1024
        ),
        cost_estimate=pl.CostEstimate(
            flops=20_000_000_000, bytes_accessed=30_000_000, transcendentals=10_000_000
        ),
        name="mixer",
    )(prompts, adv, recv, tails, wv, hv, states)


def shards(
    xbc,
    zgate,
    dt_raw,
    prompt_states,
    conv_tails,
    resp_prompt,
    resp_lengths,
    rewards,
    upstream,
    conv_weight,
    conv_bias,
    dt_bias,
    a_log,
    d_skip,
    norm_gain,
):
    dp_count = lax.axis_size("dp")
    fsdp_count = lax.axis_size("fsdp")
    dp_at = lax.axis_index("dp")
    fsdp_at = lax.axis_index("fsdp")
    docs = resp_lengths.shape[1]
    rows = xbc.shape[0]
    prompt_count, head_share = prompt_states.shape[:2]
    chan_share = conv_tails.shape[2]
    inner = DI // dp_count
    gn = GN // dp_count
    chans = inner + 2 * gn
    heads = H // dp_count

    def by_dest(a):
        return a.reshape(rows, dp_count, -1).transpose(1, 0, 2)

    hi = lax.reduce_precision(dt_raw, 8, 7)
    rest = dt_raw - hi
    mid = lax.reduce_precision(rest, 8, 7)
    low = rest - mid
    lens_cols = jnp.broadcast_to(
        resp_lengths.astype(BF16).reshape(1, 1, docs), (dp_count, rows, docs)
    )
    sent = jnp.concatenate(
        [
            by_dest(xbc[:, :DI]),
            by_dest(xbc[:, DI : DI + GN]),
            by_dest(xbc[:, DI + GN :]),
            by_dest(zgate),
            by_dest(upstream),
            by_dest(hi.astype(BF16)),
            by_dest(mid.astype(BF16)),
            by_dest(low.astype(BF16)),
            lens_cols,
            jnp.zeros((dp_count, rows, 128 - 3 * heads - docs), BF16),
        ],
        axis=2,
    )
    recv = lax.all_to_all(sent, "dp", split_axis=0, concat_axis=0, tiled=True)

    states = lax.all_gather(
        prompt_states.reshape(prompt_count, head_share * P_SIZE, N), "fsdp", axis=0
    )

    chan_w = conv_weight.shape[1]
    flat = jnp.concatenate(
        [conv_weight.reshape(-1), conv_bias, norm_gain, dt_bias, a_log, d_skip]
    )
    flat = lax.all_gather(flat, "fsdp", axis=0)
    conv_all = flat[:, : 5 * chan_w].reshape(fsdp_count, 5, chan_w).transpose(1, 0, 2)
    conv_all = conv_all.reshape(5, fsdp_count * chan_w)
    gain_w = norm_gain.shape[0]
    gain_all = flat[:, 5 * chan_w : 5 * chan_w + gain_w].reshape(-1)
    per_head = flat[:, 5 * chan_w + gain_w :].reshape(fsdp_count, 3, -1).transpose(1, 0, 2)
    per_head = lax.dynamic_slice_in_dim(per_head.reshape(3, H), dp_at * heads, heads, 1)

    def own_channels(a):
        return jnp.concatenate(
            [
                lax.dynamic_slice_in_dim(a, dp_at * inner, inner, a.ndim - 1),
                lax.dynamic_slice_in_dim(a, DI + dp_at * gn, gn, a.ndim - 1),
                lax.dynamic_slice_in_dim(a, DI + GN + dp_at * gn, gn, a.ndim - 1),
            ],
            axis=-1,
        )

    def pad_row(a):
        return jnp.pad(a, (0, chans - inner))[None]

    wv = jnp.concatenate(
        [
            own_channels(conv_all),
            pad_row(lax.dynamic_slice_in_dim(gain_all, dp_at * inner, inner)),
            pad_row(jnp.repeat(per_head[2], P_SIZE)),
            jnp.zeros((1, chans), F32),
        ]
    )
    hv = jnp.concatenate([per_head[:2], jnp.zeros((6, heads), F32)])

    holders = jnp.arange(dp_count, dtype=jnp.int32) * fsdp_count + fsdp_at
    prompts = resp_prompt.reshape(-1, docs)[holders].reshape(-1)
    adv = advantages(rewards, resp_prompt, prompt_count)
    adv = adv.reshape(-1, docs)[holders].reshape(-1)

    tails = lax.all_gather(conv_tails, ("dp", "fsdp"), axis=0)
    tails = tails.transpose(1, 2, 0, 3).reshape(prompt_count, 3, -1)
    tails = jnp.pad(own_channels(tails), ((0, 0), (0, 1), (0, 0)))
    tails = tails[prompts].reshape(dp_count, docs * 4, chans)

    out, dstate, dtail, wg = run_mixer(prompts, adv, recv, tails, wv, hv, states, docs)

    grad_states = lax.psum_scatter(dstate, "fsdp", scatter_dimension=0, tiled=False)
    grad_states = grad_states.reshape(prompt_count, head_share, P_SIZE, N)

    back = lax.all_to_all(out, "dp", split_axis=0, concat_axis=0, tiled=True)

    def home(lo, width):
        return back[:, :, lo : lo + width].transpose(1, 0, 2).reshape(rows, dp_count * width)

    grad_x = jnp.concatenate([home(0, inner), home(inner, gn), home(inner + gn, gn)], axis=1)
    grad_z = home(chans, inner)
    parts = [home(chans + inner + i * heads, heads).astype(F32) for i in range(3)]
    grad_dt = parts[0] + parts[1] + parts[2]

    onehot = (jnp.arange(prompt_count, dtype=jnp.int32)[:, None] == prompts[None, :]).astype(F32)
    dtail = dtail.reshape(dp_count * docs, 4, chans)[:, :3].reshape(dp_count * docs, 3 * chans)
    dtail = jnp.dot(onehot, dtail, precision=lax.Precision.HIGHEST)

    def spread(a, lead):
        full = jnp.zeros((lead, DI + 2 * GN), F32)
        full = lax.dynamic_update_slice(full, a[:, :inner], (0, dp_at * inner))
        full = lax.dynamic_update_slice(full, a[:, inner : inner + gn], (0, DI + dp_at * gn))
        return lax.dynamic_update_slice(full, a[:, inner + gn :], (0, DI + GN + dp_at * gn))

    tail_full = spread(dtail.reshape(prompt_count * 3, chans), prompt_count * 3)
    tail_full = tail_full.reshape(prompt_count * 3, dp_count, fsdp_count, chan_share)
    tail_full = tail_full.transpose(2, 1, 0, 3).reshape(fsdp_count, -1)
    conv_full = spread(wg[:5], 5).reshape(5, fsdp_count, chan_w).transpose(1, 0, 2)
    gain_full = lax.dynamic_update_slice(jnp.zeros((DI,), F32), wg[5, :inner], (dp_at * inner,))
    skip_grad = jnp.sum(wg[6, :inner].reshape(heads, P_SIZE), axis=1)
    head_grad = jnp.stack([wg[7, :heads], wg[8, :heads], skip_grad])
    head_full = lax.dynamic_update_slice(jnp.zeros((3, H), F32), head_grad, (0, dp_at * heads))
    head_full = head_full.reshape(3, fsdp_count, -1).transpose(1, 0, 2)
    payload = jnp.concatenate(
        [
            tail_full,
            conv_full.reshape(fsdp_count, -1),
            gain_full.reshape(fsdp_count, -1),
            head_full.reshape(fsdp_count, -1),
        ],
        axis=1,
    )
    summed = lax.psum(lax.psum_scatter(payload, "fsdp", scatter_dimension=0, tiled=False), "dp")
    tail_size = prompt_count * 3 * chan_share
    grad_tails = lax.dynamic_slice_in_dim(summed, dp_at * tail_size, tail_size)
    grad_tails = grad_tails.reshape(prompt_count, 3, chan_share)
    rest = summed[dp_count * tail_size :]
    grad_conv = rest[: 5 * chan_w].reshape(5, chan_w)
    rest = rest[5 * chan_w :]
    per = dt_bias.shape[0]
    return (
        grad_x,
        grad_z,
        grad_dt,
        grad_states,
        grad_tails,
        grad_conv[:4],
        grad_conv[4],
        rest[gain_w : gain_w + per],
        rest[gain_w + per : gain_w + 2 * per],
        rest[gain_w + 2 * per : gain_w + 3 * per],
        rest[:gain_w],
    )


def solution(mesh):
    return jax.shard_map(
        shards,
        mesh=mesh,
        in_specs=(
            P(("dp", "fsdp"), None),
            P(("dp", "fsdp"), None),
            P(("dp", "fsdp"), None),
            P(None, ("dp", "fsdp"), None, None),
            P(None, None, ("dp", "fsdp")),
            P(),
            P(("dp", "fsdp"), None),
            P(),
            P(("dp", "fsdp"), None),
            P(None, "fsdp"),
            P("fsdp"),
            P("fsdp"),
            P("fsdp"),
            P("fsdp"),
            P("fsdp"),
        ),
        out_specs=(
            P(("dp", "fsdp"), None),
            P(("dp", "fsdp"), None),
            P(("dp", "fsdp"), None),
            P(None, ("dp", "fsdp"), None, None),
            P(None, None, ("dp", "fsdp")),
            P(None, "fsdp"),
            P("fsdp"),
            P("fsdp"),
            P("fsdp"),
            P("fsdp"),
            P("fsdp"),
        ),
        check_vma=False,
    )
```

```python
import functools

import jax
import jax.numpy as jnp
from jax import lax
from jax.experimental import pallas as pl
from jax.experimental.pallas import tpu as pltpu
from jax.sharding import PartitionSpec as P

GROUP = 16
H = 128
P_SIZE = 64
N = 128
G = 8
GS = 2048
DI = H * P_SIZE
GN = G * N

CH = 256
HC = CH // P_SIZE
F32 = jnp.float32
BF16 = jnp.bfloat16
NN = (((1,), (0,)), ((), ()))
NT = (((1,), (1,)), ((), ()))


def advantages(rewards, resp_prompt, prompt_count):
    member = (resp_prompt[:, None] == jnp.arange(prompt_count, dtype=jnp.int32)[None, :]).astype(
        jnp.float32
    )
    group_mean = jnp.dot(rewards, member, precision=lax.Precision.HIGHEST) / GROUP
    centred = rewards - jnp.dot(member, group_mean, precision=lax.Precision.HIGHEST)
    spread = jnp.sqrt(jnp.dot(centred * centred, member, precision=lax.Precision.HIGHEST) / GROUP)
    return centred / jnp.dot(member, jnp.maximum(spread, 0.8), precision=lax.Precision.HIGHEST)


def dot(a, b, dims=NN):
    return lax.dot_general(a, b, dims, preferred_element_type=F32)


def split2(a):
    hi = a.astype(BF16)
    return hi, (a - hi.astype(F32)).astype(BF16)


def split3(a):
    hi = a.astype(BF16)
    rest = a - hi.astype(F32)
    mid = rest.astype(BF16)
    return hi, mid, (rest - mid.astype(F32)).astype(BF16)


def dot3(a, b, dims=NN):
    ah, al = split2(a)
    bh, bl = split2(b)
    return dot(ah, bh, dims) + dot(ah, bl, dims) + dot(al, bh, dims)


def exact_left(mask, table):
    hi, mid, lo = split3(table)
    return dot(mask, hi) + dot(mask, mid) + dot(mask, lo)


def colsum(a):
    return jnp.sum(a, axis=0, keepdims=True)


def mixer_kernel(
    dims,
    prompt_ref,
    adv_ref,
    recv_ref,
    tails_ref,
    wv_ref,
    hv_ref,
    states_ref,
    out_ref,
    dstate_ref,
    dtail_ref,
    wg_ref,
    st,
    acc,
    uext,
    co,
    dco,
    ybuf,
    sc,
    sct,
    cmh,
    cml,
    relt,
    rel3,
    se3,
    dred,
    dsc,
    dcc,
    sems,
    out_sem,
):
    rows, docs, chans, inner, heads, groups, fcount, share_rows = dims
    nf = CH // share_rows
    k = pl.program_id(0)
    inner_chunks = inner // CH
    all_chunks = chans // CH
    zoff, upoff, moff = chans, chans + inner, chans + 2 * inner
    b_off, c_off = inner, inner + groups * N

    copies = [
        pltpu.make_async_copy(states_ref.at[:, prompt_ref[k * docs + d]], st.at[d], sems.at[d])
        for d in range(docs)
    ]
    for copy in copies:
        copy.start()

    @pl.when(k == 0)
    def _():
        wg_ref[...] = jnp.zeros_like(wg_ref)
        uext[...] = jnp.zeros_like(uext)

        def clear(f, carry):
            acc[f] = jnp.zeros(acc.shape[1:], F32)
            return carry

        lax.fori_loop(0, fcount, clear, 0)

    meta = recv_ref[0, :, moff : moff + 128].astype(F32)
    lens = [meta[0:1, 96 + d : 97 + d] for d in range(docs)]
    tcol = lax.broadcasted_iota(jnp.int32, (rows, 1), 0).astype(F32)
    trow = lax.broadcasted_iota(jnp.int32, (1, rows), 1).astype(F32)
    doc_col, doc_row = jnp.zeros_like(tcol), jnp.zeros_like(trow)
    start_col, start_row = jnp.zeros_like(tcol), jnp.zeros_like(trow)
    begin = jnp.zeros((1, 1), F32)
    for d in range(docs - 1):
        begin = begin + lens[d]
        doc_col = doc_col + jnp.where(tcol >= begin, 1.0, 0.0)
        doc_row = doc_row + jnp.where(trow >= begin, 1.0, 0.0)
        start_col = jnp.where(tcol >= begin, begin, start_col)
        start_row = jnp.where(trow >= begin, begin, start_row)
    off_col, off_row = tcol - start_col, trow - start_row
    wtok = jnp.zeros_like(tcol)
    for d in range(docs):
        wtok = wtok + jnp.where(
            doc_col == d, adv_ref[k * docs + d] * (rows / (docs * lens[d])), 0.0
        )
    same = doc_col == doc_row
    causal = same & (tcol >= trow)
    causal_t = same & (trow >= tcol)

    ext_row = lax.broadcasted_iota(jnp.int32, (1, 2 * rows), 1).astype(F32)
    ext_col = lax.broadcasted_iota(jnp.int32, (rows + 16, 1), 0).astype(F32)
    shift, shift_t = [], []
    for j in (1, 2, 3):
        src_col = jnp.where(off_col >= j, tcol - j, rows + doc_col * 4 + (3 - j) + off_col)
        src_row = jnp.where(off_row >= j, trow - j, rows + doc_row * 4 + (3 - j) + off_row)
        shift.append(jnp.where(src_col == ext_row, 1.0, 0.0).astype(BF16))
        shift_t.append(jnp.where(src_row == ext_col, 1.0, 0.0).astype(BF16))
    shift = jnp.concatenate(shift, axis=0)
    shift_t = jnp.concatenate(shift_t, axis=1)

    uext[0:rows, :] = recv_ref[0, :, 0:chans]
    uext[rows : rows + 16, :] = tails_ref[0]

    def conv(cs):
        u = uext[:, pl.ds(cs, CH)]
        lag = dot(shift, u)
        taps = [u[0:rows].astype(F32)] + [lag[i * rows : (i + 1) * rows] for i in range(3)]
        w = [wv_ref[3 - j : 4 - j, pl.ds(cs, CH)] for j in range(4)]
        pre = wv_ref[4:5, pl.ds(cs, CH)] + sum(w[j] * taps[j] for j in range(4))
        return pre, taps, w

    def conv_step(i, carry):
        cs = pl.multiple_of(i * CH, CH)
        pre, _, _ = conv(cs)
        co[:, pl.ds(cs, CH)] = pre * jax.nn.sigmoid(pre)
        return carry

    lax.fori_loop(0, all_chunks, conv_step, 0)

    for g in range(groups):
        bg = co[:, b_off + g * N : b_off + (g + 1) * N]
        cg = co[:, c_off + g * N : c_off + (g + 1) * N]
        sc[g] = dot3(cg, bg, NT)
        sct[g] = dot3(bg, cg, NT)
        hi, lo = split2(cg)
        zero = jnp.zeros_like(hi)
        for d in range(docs):
            cmh[g, :, d * N : (d + 1) * N] = jnp.where(doc_col == d, hi, zero)
            cml[g, :, d * N : (d + 1) * N] = jnp.where(doc_col == d, lo, zero)
        dsc[g] = jnp.zeros((rows, rows), F32)
        dcc[g] = jnp.zeros((rows, N), F32)
    dred[...] = jnp.zeros_like(dred)

    dt_pre = meta[:, 0:32] + meta[:, 32:64] + meta[:, 64:96] + hv_ref[0:1, :]
    tail_exp = jnp.exp(-jnp.abs(dt_pre))
    step = jnp.maximum(dt_pre, 0.0) + jnp.log1p(tail_exp)
    rate = -jnp.exp(hv_ref[1:2, :])
    dec = step * rate
    rel = exact_left(jnp.where(causal, 1.0, 0.0).astype(BF16), dec)
    relt[...] = rel.T
    rel3[...] = jnp.concatenate(split3(rel), axis=1)
    se3[0:rows, :] = jnp.concatenate(split3(step), axis=1)
    se3[rows : 2 * rows, :] = jnp.concatenate(split3(jnp.exp(rel)), axis=1)

    def head_onehot(c, width):
        r = lax.broadcasted_iota(jnp.int32, (3 * heads, HC * width), 0)
        r = jnp.where(r >= 2 * heads, r - 2 * heads, jnp.where(r >= heads, r - heads, r))
        lane = lax.broadcasted_iota(jnp.int32, (3 * heads, HC * width), 1)
        return jnp.where(r == c * HC + lane // width, 1.0, 0.0).astype(BF16)

    lane_head = lax.broadcasted_iota(jnp.int32, (1, CH), 1) // P_SIZE

    def block_diag(a):
        zero = jnp.zeros_like(a)
        return jnp.concatenate([jnp.where(lane_head == h, a, zero) for h in range(HC)], axis=0)

    def chunk_tables(c):
        expand = dot(se3[...], head_onehot(c, P_SIZE))
        colb = dot(rel3[...], head_onehot(c, rows))
        rowb = [relt[pl.ds(c * HC + h, 1), :] for h in range(HC)]
        return expand[0:rows], expand[rows : 2 * rows], colb, rowb

    def state_of(d, c):
        return st[d, pl.ds(c * nf, nf)].reshape(CH, N)

    for copy in copies:
        copy.wait()

    def forward_step(c, carry):
        s1, s2 = carry
        cs = pl.multiple_of(c * CH, CH)
        g = c // (inner_chunks // groups)
        stepx, ex, colb, rowb = chunk_tables(c)
        x = co[:, pl.ds(cs, CH)]
        xh, xl = split2(x * stepx)
        score = sc[g]
        w = jnp.concatenate(
            [
                jnp.exp(jnp.where(causal, colb[:, h * rows : (h + 1) * rows] - rowb[h], -1e30))
                * score
                for h in range(HC)
            ],
            axis=1,
        )
        wh, wl = split2(w)
        bh, bl = block_diag(xh), block_diag(xl)
        within = dot(wh, bh) + dot(wh, bl) + dot(wl, bh)
        carried = jnp.zeros((rows, CH), F32)
        for d in range(docs):
            state = state_of(d, c)
            carried = carried + dot(cmh[g, :, d * N : (d + 1) * N], state, NT)
            carried = carried + dot(cml[g, :, d * N : (d + 1) * N], state, NT)
        y = within + ex * carried + wv_ref[6:7, pl.ds(cs, CH)] * x
        ybuf[:, pl.ds(cs, CH)] = y
        z = recv_ref[0, :, pl.ds(zoff + cs, CH)].astype(F32)
        up = recv_ref[0, :, pl.ds(upoff + cs, CH)].astype(F32)
        v = y * (z * jax.nn.sigmoid(z))
        p1 = v * v
        p2 = up * wv_ref[5:6, pl.ds(cs, CH)] * v
        return s1 + p1[:, :128] + p1[:, 128:], s2 + p2[:, :128] + p2[:, 128:]

    zeros = jnp.zeros((rows, 128), F32)
    s1, s2 = lax.fori_loop(0, inner_chunks, forward_step, (zeros, zeros))
    inv = lax.rsqrt(jnp.sum(s1, axis=1, keepdims=True) / GS + 1e-05)
    mean2 = jnp.sum(s2, axis=1, keepdims=True) * wtok / GS
    coef = inv * inv * inv * mean2

    def backward_step(c, carry):
        cs = pl.multiple_of(c * CH, CH)
        g = c // (inner_chunks // groups)
        stepx, ex, colb, rowb = chunk_tables(c)
        x = co[:, pl.ds(cs, CH)]
        y = ybuf[:, pl.ds(cs, CH)]
        z = recv_ref[0, :, pl.ds(zoff + cs, CH)].astype(F32)
        up = recv_ref[0, :, pl.ds(upoff + cs, CH)].astype(F32)
        skip = wv_ref[6:7, pl.ds(cs, CH)]
        sg = jax.nn.sigmoid(z)
        sz = z * sg
        v = y * sz
        dn = up * (wtok * inv)
        wg_ref[5:6, pl.ds(cs, CH)] += colsum(dn * v)
        dv = dn * wv_ref[5:6, pl.ds(cs, CH)] - v * coef
        dy = dv * sz
        out_ref[0, :, pl.ds(chans + cs, CH)] = (dv * y * (sg * (1.0 + z * (1.0 - sg)))).astype(
            BF16
        )
        xs = x * stepx
        xh, xl = split2(xs)
        dyh, dyl = split2(dy)
        bh, bl = block_diag(xh), block_diag(xl)
        dm = dot(dyh, bh, NT) + dot(dyh, bl, NT) + dot(dyl, bh, NT)
        score_t = sct[g]
        total = dsc[g]
        wt = []
        for h in range(HC):
            gap = colb[:, h * rows : (h + 1) * rows] - rowb[h]
            total = total + jnp.exp(jnp.where(causal, gap, -1e30)) * dm[:, h * rows : (h + 1) * rows]
            wt.append(jnp.exp(jnp.where(causal_t, -gap, -1e30)) * score_t)
        dsc[g] = total
        wh, wl = split2(jnp.concatenate(wt, axis=1))
        dh, dl = block_diag(dyh), block_diag(dyl)
        dxs = dot(wh, dh) + dot(wh, dl) + dot(wl, dh)
        dco[:, pl.ds(cs, CH)] = stepx * dxs + skip * dy
        wg_ref[6:7, pl.ds(cs, CH)] += colsum(dy * x)
        both = jnp.concatenate([dy * (y - skip * x) - xs * dxs, dxs * x], axis=0)
        pick = jnp.where(
            lax.broadcasted_iota(jnp.int32, (CH, heads), 0) // P_SIZE + c * HC
            == lax.broadcasted_iota(jnp.int32, (CH, heads), 1),
            1.0,
            0.0,
        ).astype(BF16)
        b1, b2, b3 = split3(both)
        dred[...] += dot(b1, pick) + dot(b2, pick) + dot(b3, pick)
        q = ex * dy
        qh, ql = split2(q)
        qth, qtl = split2(q.T)
        ch, cl = cmh[g], cml[g]
        ds_all = dot(qth, ch) + dot(qtl, ch) + dot(qth, cl)
        back = jnp.zeros((rows, N), F32)
        for d in range(docs):
            p = prompt_ref[k * docs + d]
            acc[pl.ds(c * nf, nf), p] += ds_all[:, d * N : (d + 1) * N].reshape(nf, share_rows, N)
            state = state_of(d, c)
            back = back + jnp.where(doc_col == d, dot(qh, state) + dot(ql, state), 0.0)
        dcc[g] += back
        return carry

    lax.fori_loop(0, inner_chunks, backward_step, 0)

    @pl.when(k == pl.num_programs(0) - 1)
    def _():
        pltpu.make_async_copy(acc, dstate_ref, out_sem).start()

    for g in range(groups):
        bg = co[:, b_off + g * N : b_off + (g + 1) * N]
        cg = co[:, c_off + g * N : c_off + (g + 1) * N]
        dco[:, c_off + g * N : c_off + (g + 1) * N] = dot3(dsc[g], bg) + dcc[g]
        dco[:, b_off + g * N : b_off + (g + 1) * N] = dot3(dsc[g].T, cg)

    ddec = exact_left(jnp.where(causal_t, 1.0, 0.0).astype(BF16), dred[0:rows])
    ddt = (dred[rows : 2 * rows] + ddec * rate) * jax.nn.sigmoid(dt_pre)
    wg_ref[7:8, 0:heads] += colsum(ddt)
    wg_ref[8:9, 0:heads] += colsum(ddec * dec)
    out_ref[0, :, chans + inner :] = jnp.concatenate(
        list(split3(ddt)) + [jnp.zeros((rows, 128 - 3 * heads), BF16)], axis=1
    )

    def conv_back(i, carry):
        cs = pl.multiple_of(i * CH, CH)
        pre, taps, w = conv(cs)
        sg = jax.nn.sigmoid(pre)
        dpre = dco[:, pl.ds(cs, CH)] * (sg * (1.0 + pre * (1.0 - sg)))
        for j in range(4):
            wg_ref[3 - j : 4 - j, pl.ds(cs, CH)] += colsum(dpre * taps[j])
        wg_ref[4:5, pl.ds(cs, CH)] += colsum(dpre)
        hi, lo = split2(jnp.concatenate([w[j] * dpre for j in (1, 2, 3)], axis=0))
        du = dot(shift_t, hi) + dot(shift_t, lo)
        out_ref[0, :, pl.ds(cs, CH)] = (w[0] * dpre + du[0:rows]).astype(BF16)
        dtail_ref[0, :, pl.ds(cs, CH)] = du[rows : rows + 16]
        return carry

    lax.fori_loop(0, all_chunks, conv_back, 0)

    @pl.when(k == pl.num_programs(0) - 1)
    def _():
        pltpu.make_async_copy(acc, dstate_ref, out_sem).wait()


def run_mixer(prompts, adv, recv, tails, wv, hv, states, docs):
    blocks, rows, width = recv.shape
    chans = wv.shape[1]
    fcount, prompt_count, share_rows, _ = states.shape
    inner = fcount * share_rows
    heads = inner // P_SIZE
    groups = (chans - inner) // (2 * N)
    dims = (rows, docs, chans, inner, heads, groups, fcount, share_rows)
    out_width = chans + inner + 128
    smem = pl.BlockSpec(memory_space=pltpu.SMEM)
    hbm = pl.BlockSpec(memory_space=pl.ANY)
    return pl.pallas_call(
        functools.partial(mixer_kernel, dims),
        grid=(blocks,),
        in_specs=[
            smem,
            smem,
            pl.BlockSpec((1, rows, width), lambda i: (i, 0, 0)),
            pl.BlockSpec((1, 16, chans), lambda i: (i, 0, 0)),
            pl.BlockSpec(wv.shape, lambda i: (0, 0)),
            pl.BlockSpec(hv.shape, lambda i: (0, 0)),
            hbm,
        ],
        out_specs=[
            pl.BlockSpec((1, rows, out_width), lambda i: (i, 0, 0)),
            hbm,
            pl.BlockSpec((1, 16, chans), lambda i: (i, 0, 0)),
            pl.BlockSpec((16, chans), lambda i: (0, 0)),
        ],
        out_shape=[
            jax.ShapeDtypeStruct((blocks, rows, out_width), BF16),
            jax.ShapeDtypeStruct(states.shape, F32),
            jax.ShapeDtypeStruct((blocks, 16, chans), F32),
            jax.ShapeDtypeStruct((16, chans), F32),
        ],
        scratch_shapes=[
            pltpu.VMEM((docs, fcount, share_rows, N), BF16),
            pltpu.VMEM(states.shape, F32),
            pltpu.VMEM((2 * rows, chans), BF16),
            pltpu.VMEM((rows, chans), F32),
            pltpu.VMEM((rows, chans), F32),
            pltpu.VMEM((rows, inner), F32),
            pltpu.VMEM((groups, rows, rows), F32),
            pltpu.VMEM((groups, rows, rows), F32),
            pltpu.VMEM((groups, rows, docs * N), BF16),
            pltpu.VMEM((groups, rows, docs * N), BF16),
            pltpu.VMEM((heads, rows), F32),
            pltpu.VMEM((rows, 3 * heads), BF16),
            pltpu.VMEM((2 * rows, 3 * heads), BF16),
            pltpu.VMEM((2 * rows, heads), F32),
            pltpu.VMEM((groups, rows, rows), F32),
            pltpu.VMEM((groups, rows, N), F32),
            pltpu.SemaphoreType.DMA((docs,)),
            pltpu.SemaphoreType.DMA,
        ],
        compiler_params=pltpu.CompilerParams(
            dimension_semantics=("arbitrary",), vmem_limit_bytes=60 * 1024 * 1024
        ),
        cost_estimate=pl.CostEstimate(
            flops=20_000_000_000, bytes_accessed=30_000_000, transcendentals=10_000_000
        ),
        name="mixer",
    )(prompts, adv, recv, tails, wv, hv, states)


def pack_kernel(dims, xp, bp, cp, zp, upp, dtp, lenp, out):
    inner, gn, heads, docs = dims
    rows = xp.shape[0]
    i = pl.program_id(0)
    at = 0
    for ref in (xp, bp, cp, zp, upp):
        width = ref.shape[1]
        out[0, :, at : at + width] = ref[...]
        at += width
    lane = lax.broadcasted_iota(jnp.int32, (1, dtp.shape[1]), 1) // heads
    own = jnp.where(lane == i, dtp[...], 0.0)
    dt = sum(own[:, j * heads : (j + 1) * heads] for j in range(dtp.shape[1] // heads))
    lens = jnp.broadcast_to(lenp[...].astype(F32), (rows, docs)).astype(BF16)
    pad = jnp.zeros((rows, 128 - 3 * heads - docs), BF16)
    out[0, :, at:] = jnp.concatenate(list(split3(dt)) + [lens, pad], axis=1)


def pack(xbc, zgate, upstream, dt_raw, resp_lengths, dp_count):
    rows = xbc.shape[0]
    docs = resp_lengths.shape[1]
    inner, gn, heads = DI // dp_count, GN // dp_count, H // dp_count
    width = 3 * inner + 2 * gn + 128
    return pl.pallas_call(
        functools.partial(pack_kernel, (inner, gn, heads, docs)),
        grid=(dp_count,),
        in_specs=[
            pl.BlockSpec((rows, inner), lambda i: (0, i)),
            pl.BlockSpec((rows, gn), lambda i: (0, DI // gn + i)),
            pl.BlockSpec((rows, gn), lambda i: (0, (DI + GN) // gn + i)),
            pl.BlockSpec((rows, inner), lambda i: (0, i)),
            pl.BlockSpec((rows, inner), lambda i: (0, i)),
            pl.BlockSpec(dt_raw.shape, lambda i: (0, 0)),
            pl.BlockSpec(resp_lengths.shape, lambda i: (0, 0)),
        ],
        out_specs=pl.BlockSpec((1, rows, width), lambda i: (i, 0, 0)),
        out_shape=jax.ShapeDtypeStruct((dp_count, rows, width), BF16),
        compiler_params=pltpu.CompilerParams(
            dimension_semantics=("arbitrary",), vmem_limit_bytes=32 * 1024 * 1024
        ),
        name="pack",
    )(xbc, xbc, xbc, zgate, upstream, dt_raw, resp_lengths)


def unpack_kernel(dims, back, gx, gz, gdt):
    inner, gn, heads = dims
    i = pl.program_id(0)
    gx[:, pl.ds(pl.multiple_of(i * inner, inner), inner)] = back[0, :, 0:inner]
    gx[:, pl.ds(pl.multiple_of(DI + i * gn, gn), gn)] = back[0, :, inner : inner + gn]
    gx[:, pl.ds(pl.multiple_of(DI + GN + i * gn, gn), gn)] = back[
        0, :, inner + gn : inner + 2 * gn
    ]
    gz[...] = back[0, :, inner + 2 * gn : 2 * inner + 2 * gn]
    meta = back[0, :, 2 * inner + 2 * gn :].astype(F32)
    dt = meta[:, 0:heads] + meta[:, heads : 2 * heads] + meta[:, 2 * heads : 3 * heads]
    wide = jnp.concatenate([dt] * (H // heads), axis=1)
    lane = lax.broadcasted_iota(jnp.int32, (1, H), 1) // heads
    gdt[...] = jnp.where(lane == i, wide, gdt[...])


def unpack(back):
    dp_count, rows, width = back.shape
    inner, gn, heads = DI // dp_count, GN // dp_count, H // dp_count
    return pl.pallas_call(
        functools.partial(unpack_kernel, (inner, gn, heads)),
        grid=(dp_count,),
        in_specs=[pl.BlockSpec((1, rows, width), lambda i: (i, 0, 0))],
        out_specs=[
            pl.BlockSpec((rows, DI + 2 * GN), lambda i: (0, 0)),
            pl.BlockSpec((rows, inner), lambda i: (0, i)),
            pl.BlockSpec((rows, H), lambda i: (0, 0)),
        ],
        out_shape=[
            jax.ShapeDtypeStruct((rows, DI + 2 * GN), BF16),
            jax.ShapeDtypeStruct((rows, DI), BF16),
            jax.ShapeDtypeStruct((rows, H), F32),
        ],
        compiler_params=pltpu.CompilerParams(
            dimension_semantics=("arbitrary",), vmem_limit_bytes=32 * 1024 * 1024
        ),
        name="unpack",
    )(back)


def to_all(a, axes, count):
    many = jnp.broadcast_to(a[None], (count,) + a.shape)
    return lax.all_to_all(many, axes, split_axis=0, concat_axis=0, tiled=True)


def shards(
    xbc,
    zgate,
    dt_raw,
    prompt_states,
    conv_tails,
    resp_prompt,
    resp_lengths,
    rewards,
    upstream,
    conv_weight,
    conv_bias,
    dt_bias,
    a_log,
    d_skip,
    norm_gain,
):
    dp_count = lax.axis_size("dp")
    fsdp_count = lax.axis_size("fsdp")
    dp_at = lax.axis_index("dp")
    fsdp_at = lax.axis_index("fsdp")
    docs = resp_lengths.shape[1]
    rows = xbc.shape[0]
    prompt_count, head_share = prompt_states.shape[:2]
    chan_share = conv_tails.shape[2]
    inner = DI // dp_count
    gn = GN // dp_count
    chans = inner + 2 * gn
    heads = H // dp_count

    sent = pack(xbc, zgate, upstream, dt_raw, resp_lengths, dp_count)
    recv = lax.all_to_all(sent, "dp", split_axis=0, concat_axis=0, tiled=True)

    states = lax.all_gather(
        prompt_states.reshape(prompt_count, head_share * P_SIZE, N), "fsdp", axis=0
    )

    chan_w = conv_weight.shape[1]
    flat = jnp.concatenate(
        [conv_weight.reshape(-1), conv_bias, norm_gain, dt_bias, a_log, d_skip]
    )
    flat = to_all(flat, "fsdp", fsdp_count)
    conv_all = flat[:, : 5 * chan_w].reshape(fsdp_count, 5, chan_w).transpose(1, 0, 2)
    conv_all = conv_all.reshape(5, fsdp_count * chan_w)
    gain_w = norm_gain.shape[0]
    gain_all = flat[:, 5 * chan_w : 5 * chan_w + gain_w].reshape(-1)
    per_head = flat[:, 5 * chan_w + gain_w :].reshape(fsdp_count, 3, -1).transpose(1, 0, 2)
    per_head = lax.dynamic_slice_in_dim(per_head.reshape(3, H), dp_at * heads, heads, 1)

    def own_channels(a):
        return jnp.concatenate(
            [
                lax.dynamic_slice_in_dim(a, dp_at * inner, inner, a.ndim - 1),
                lax.dynamic_slice_in_dim(a, DI + dp_at * gn, gn, a.ndim - 1),
                lax.dynamic_slice_in_dim(a, DI + GN + dp_at * gn, gn, a.ndim - 1),
            ],
            axis=-1,
        )

    def pad_row(a):
        return jnp.pad(a, (0, chans - inner))[None]

    wv = jnp.concatenate(
        [
            own_channels(conv_all),
            pad_row(lax.dynamic_slice_in_dim(gain_all, dp_at * inner, inner)),
            pad_row(jnp.repeat(per_head[2], P_SIZE)),
            jnp.zeros((1, chans), F32),
        ]
    )
    hv = jnp.concatenate([per_head[:2], jnp.zeros((6, heads), F32)])

    holders = jnp.arange(dp_count, dtype=jnp.int32) * fsdp_count + fsdp_at
    prompts = resp_prompt.reshape(-1, docs)[holders].reshape(-1)
    adv = advantages(rewards, resp_prompt, prompt_count)
    adv = adv.reshape(-1, docs)[holders].reshape(-1)

    tails = to_all(conv_tails, ("dp", "fsdp"), dp_count * fsdp_count)
    tails = tails.transpose(1, 2, 0, 3).reshape(prompt_count, 3, -1)
    tails = jnp.pad(own_channels(tails), ((0, 0), (0, 1), (0, 0)))
    tails = tails[prompts].reshape(dp_count, docs * 4, chans)

    out, dstate, dtail, wg = run_mixer(prompts, adv, recv, tails, wv, hv, states, docs)

    grad_states = lax.psum_scatter(dstate, "fsdp", scatter_dimension=0, tiled=False)
    grad_states = grad_states.reshape(prompt_count, head_share, P_SIZE, N)

    back = lax.all_to_all(out, "dp", split_axis=0, concat_axis=0, tiled=True)

    grad_x, grad_z, grad_dt = unpack(back)

    onehot = (jnp.arange(prompt_count, dtype=jnp.int32)[:, None] == prompts[None, :]).astype(F32)
    dtail = dtail.reshape(dp_count * docs, 4, chans)[:, :3].reshape(dp_count * docs, 3 * chans)
    dtail = jnp.dot(onehot, dtail, precision=lax.Precision.HIGHEST)

    def spread(a, lead):
        full = jnp.zeros((lead, DI + 2 * GN), F32)
        full = lax.dynamic_update_slice(full, a[:, :inner], (0, dp_at * inner))
        full = lax.dynamic_update_slice(full, a[:, inner : inner + gn], (0, DI + dp_at * gn))
        return lax.dynamic_update_slice(full, a[:, inner + gn :], (0, DI + GN + dp_at * gn))

    tail_full = spread(dtail.reshape(prompt_count * 3, chans), prompt_count * 3)
    tail_full = tail_full.reshape(prompt_count * 3, dp_count, fsdp_count, chan_share)
    tail_full = tail_full.transpose(2, 1, 0, 3).reshape(fsdp_count, -1)
    conv_full = spread(wg[:5], 5).reshape(5, fsdp_count, chan_w).transpose(1, 0, 2)
    gain_full = lax.dynamic_update_slice(jnp.zeros((DI,), F32), wg[5, :inner], (dp_at * inner,))
    skip_grad = jnp.sum(wg[6, :inner].reshape(heads, P_SIZE), axis=1)
    head_grad = jnp.stack([wg[7, :heads], wg[8, :heads], skip_grad])
    head_full = lax.dynamic_update_slice(jnp.zeros((3, H), F32), head_grad, (0, dp_at * heads))
    head_full = head_full.reshape(3, fsdp_count, -1).transpose(1, 0, 2)
    payload = jnp.concatenate(
        [
            tail_full,
            conv_full.reshape(fsdp_count, -1),
            gain_full.reshape(fsdp_count, -1),
            head_full.reshape(fsdp_count, -1),
        ],
        axis=1,
    )
    summed = jnp.sum(lax.all_to_all(payload, "fsdp", split_axis=0, concat_axis=0, tiled=True), axis=0)
    tail_size = prompt_count * 3 * chan_share
    shared = summed[dp_count * tail_size :]
    pieces = jnp.concatenate(
        [
            summed[: dp_count * tail_size].reshape(dp_count, tail_size),
            jnp.broadcast_to(shared[None], (dp_count,) + shared.shape),
        ],
        axis=1,
    )
    summed = jnp.sum(lax.all_to_all(pieces, "dp", split_axis=0, concat_axis=0, tiled=True), axis=0)
    grad_tails = summed[:tail_size].reshape(prompt_count, 3, chan_share)
    rest = summed[tail_size:]
    grad_conv = rest[: 5 * chan_w].reshape(5, chan_w)
    rest = rest[5 * chan_w :]
    per = dt_bias.shape[0]
    return (
        grad_x,
        grad_z,
        grad_dt,
        grad_states,
        grad_tails,
        grad_conv[:4],
        grad_conv[4],
        rest[gain_w : gain_w + per],
        rest[gain_w + per : gain_w + 2 * per],
        rest[gain_w + 2 * per : gain_w + 3 * per],
        rest[:gain_w],
    )


def solution(mesh):
    return jax.shard_map(
        shards,
        mesh=mesh,
        in_specs=(
            P(("dp", "fsdp"), None),
            P(("dp", "fsdp"), None),
            P(("dp", "fsdp"), None),
            P(None, ("dp", "fsdp"), None, None),
            P(None, None, ("dp", "fsdp")),
            P(),
            P(("dp", "fsdp"), None),
            P(),
            P(("dp", "fsdp"), None),
            P(None, "fsdp"),
            P("fsdp"),
            P("fsdp"),
            P("fsdp"),
            P("fsdp"),
            P("fsdp"),
        ),
        out_specs=(
            P(("dp", "fsdp"), None),
            P(("dp", "fsdp"), None),
            P(("dp", "fsdp"), None),
            P(None, ("dp", "fsdp"), None, None),
            P(None, None, ("dp", "fsdp")),
            P(None, "fsdp"),
            P("fsdp"),
            P("fsdp"),
            P("fsdp"),
            P("fsdp"),
            P("fsdp"),
        ),
        check_vma=False,
    )
```

```python
import functools

import jax
import jax.numpy as jnp
from jax import lax
from jax.experimental import pallas as pl
from jax.experimental.pallas import tpu as pltpu
from jax.sharding import PartitionSpec as P

GROUP = 16
H = 128
P_SIZE = 64
N = 128
G = 8
GS = 2048
DI = H * P_SIZE
GN = G * N

CH = 256
HC = CH // P_SIZE
F32 = jnp.float32
BF16 = jnp.bfloat16
NN = (((1,), (0,)), ((), ()))
NT = (((1,), (1,)), ((), ()))


def advantages(rewards, resp_prompt, prompt_count):
    member = (resp_prompt[:, None] == jnp.arange(prompt_count, dtype=jnp.int32)[None, :]).astype(
        jnp.float32
    )
    group_mean = jnp.dot(rewards, member, precision=lax.Precision.HIGHEST) / GROUP
    centred = rewards - jnp.dot(member, group_mean, precision=lax.Precision.HIGHEST)
    spread = jnp.sqrt(jnp.dot(centred * centred, member, precision=lax.Precision.HIGHEST) / GROUP)
    return centred / jnp.dot(member, jnp.maximum(spread, 0.8), precision=lax.Precision.HIGHEST)


def dot(a, b, dims=NN):
    return lax.dot_general(a, b, dims, preferred_element_type=F32)


def split2(a):
    hi = a.astype(BF16)
    return hi, (a - hi.astype(F32)).astype(BF16)


def split3(a):
    hi = a.astype(BF16)
    rest = a - hi.astype(F32)
    mid = rest.astype(BF16)
    return hi, mid, (rest - mid.astype(F32)).astype(BF16)


def dot3(a, b, dims=NN):
    ah, al = split2(a)
    bh, bl = split2(b)
    return dot(ah, bh, dims) + dot(ah, bl, dims) + dot(al, bh, dims)


def exact_left(mask, table):
    hi, mid, lo = split3(table)
    return dot(mask, hi) + dot(mask, mid) + dot(mask, lo)


def colsum(a):
    return jnp.sum(a, axis=0, keepdims=True)


def mixer_kernel(
    dims,
    prompt_ref,
    adv_ref,
    recv_ref,
    tails_ref,
    wv_ref,
    hv_ref,
    states_ref,
    out_ref,
    dstate_ref,
    dtail_ref,
    wg_ref,
    st,
    acc,
    uext,
    co,
    dco,
    ybuf,
    sc,
    sct,
    cmh,
    cml,
    relt,
    rel3,
    se3,
    dred,
    dsc,
    dcc,
    sems,
    out_sem,
):
    rows, docs, chans, inner, heads, groups, fcount, share_rows = dims
    nf = CH // share_rows
    k = pl.program_id(0)
    inner_chunks = inner // CH
    all_chunks = chans // CH
    zoff, upoff, moff = chans, chans + inner, chans + 2 * inner
    b_off, c_off = inner, inner + groups * N

    copies = [
        pltpu.make_async_copy(states_ref.at[:, prompt_ref[k * docs + d]], st.at[d], sems.at[d])
        for d in range(docs)
    ]
    for copy in copies:
        copy.start()

    @pl.when(k == 0)
    def _():
        wg_ref[...] = jnp.zeros_like(wg_ref)
        uext[...] = jnp.zeros_like(uext)

        def clear(f, carry):
            acc[f] = jnp.zeros(acc.shape[1:], F32)
            return carry

        lax.fori_loop(0, fcount, clear, 0)

    meta = recv_ref[0, :, moff : moff + 128].astype(F32)
    lens = [meta[0:1, 96 + d : 97 + d] for d in range(docs)]
    tcol = lax.broadcasted_iota(jnp.int32, (rows, 1), 0).astype(F32)
    trow = lax.broadcasted_iota(jnp.int32, (1, rows), 1).astype(F32)
    doc_col, doc_row = jnp.zeros_like(tcol), jnp.zeros_like(trow)
    start_col, start_row = jnp.zeros_like(tcol), jnp.zeros_like(trow)
    begin = jnp.zeros((1, 1), F32)
    for d in range(docs - 1):
        begin = begin + lens[d]
        doc_col = doc_col + jnp.where(tcol >= begin, 1.0, 0.0)
        doc_row = doc_row + jnp.where(trow >= begin, 1.0, 0.0)
        start_col = jnp.where(tcol >= begin, begin, start_col)
        start_row = jnp.where(trow >= begin, begin, start_row)
    off_col, off_row = tcol - start_col, trow - start_row
    wtok = jnp.zeros_like(tcol)
    for d in range(docs):
        wtok = wtok + jnp.where(
            doc_col == d, adv_ref[k * docs + d] * (rows / (docs * lens[d])), 0.0
        )
    same = doc_col == doc_row
    causal = same & (tcol >= trow)
    causal_t = same & (trow >= tcol)

    ext_row = lax.broadcasted_iota(jnp.int32, (1, 2 * rows), 1).astype(F32)
    ext_col = lax.broadcasted_iota(jnp.int32, (rows + 16, 1), 0).astype(F32)
    shift, shift_t = [], []
    for j in (1, 2, 3):
        src_col = jnp.where(off_col >= j, tcol - j, rows + doc_col * 4 + (3 - j) + off_col)
        src_row = jnp.where(off_row >= j, trow - j, rows + doc_row * 4 + (3 - j) + off_row)
        shift.append(jnp.where(src_col == ext_row, 1.0, 0.0).astype(BF16))
        shift_t.append(jnp.where(src_row == ext_col, 1.0, 0.0).astype(BF16))
    shift = jnp.concatenate(shift, axis=0)
    shift_t = jnp.concatenate(shift_t, axis=1)

    uext[0:rows, :] = recv_ref[0, :, 0:chans]
    uext[rows : rows + 16, :] = tails_ref[0]

    def conv(cs):
        u = uext[:, pl.ds(cs, CH)]
        lag = dot(shift, u)
        taps = [u[0:rows].astype(F32)] + [lag[i * rows : (i + 1) * rows] for i in range(3)]
        w = [wv_ref[3 - j : 4 - j, pl.ds(cs, CH)] for j in range(4)]
        pre = wv_ref[4:5, pl.ds(cs, CH)] + sum(w[j] * taps[j] for j in range(4))
        return pre, taps, w

    def conv_step(i, carry):
        cs = pl.multiple_of(i * CH, CH)
        pre, _, _ = conv(cs)
        co[:, pl.ds(cs, CH)] = pre * jax.nn.sigmoid(pre)
        return carry

    lax.fori_loop(0, all_chunks, conv_step, 0)

    for g in range(groups):
        bg = co[:, b_off + g * N : b_off + (g + 1) * N]
        cg = co[:, c_off + g * N : c_off + (g + 1) * N]
        sc[g] = dot3(cg, bg, NT)
        sct[g] = dot3(bg, cg, NT)
        hi, lo = split2(cg)
        zero = jnp.zeros_like(hi)
        for d in range(docs):
            cmh[g, :, d * N : (d + 1) * N] = jnp.where(doc_col == d, hi, zero)
            cml[g, :, d * N : (d + 1) * N] = jnp.where(doc_col == d, lo, zero)
        dsc[g] = jnp.zeros((rows, rows), F32)
        dcc[g] = jnp.zeros((rows, N), F32)
    dred[...] = jnp.zeros_like(dred)

    dt_pre = meta[:, 0:32] + meta[:, 32:64] + meta[:, 64:96] + hv_ref[0:1, :]
    tail_exp = jnp.exp(-jnp.abs(dt_pre))
    step = jnp.maximum(dt_pre, 0.0) + jnp.log1p(tail_exp)
    rate = -jnp.exp(hv_ref[1:2, :])
    dec = step * rate
    rel = exact_left(jnp.where(causal, 1.0, 0.0).astype(BF16), dec)
    relt[...] = rel.T
    rel3[...] = jnp.concatenate(split3(rel), axis=1)
    se3[0:rows, :] = jnp.concatenate(split3(step), axis=1)
    se3[rows : 2 * rows, :] = jnp.concatenate(split3(jnp.exp(rel)), axis=1)

    def head_onehot(c, width):
        r = lax.broadcasted_iota(jnp.int32, (3 * heads, HC * width), 0)
        r = jnp.where(r >= 2 * heads, r - 2 * heads, jnp.where(r >= heads, r - heads, r))
        lane = lax.broadcasted_iota(jnp.int32, (3 * heads, HC * width), 1)
        return jnp.where(r == c * HC + lane // width, 1.0, 0.0).astype(BF16)

    lane_head = lax.broadcasted_iota(jnp.int32, (1, CH), 1) // P_SIZE

    def block_diag(a):
        zero = jnp.zeros_like(a)
        return jnp.concatenate([jnp.where(lane_head == h, a, zero) for h in range(HC)], axis=0)

    def chunk_tables(c):
        expand = dot(se3[...], head_onehot(c, P_SIZE))
        colb = dot(rel3[...], head_onehot(c, rows))
        rowb = [relt[pl.ds(c * HC + h, 1), :] for h in range(HC)]
        return expand[0:rows], expand[rows : 2 * rows], colb, rowb

    def state_of(d, c):
        return st[d, pl.ds(c * nf, nf)].reshape(CH, N)

    for copy in copies:
        copy.wait()

    def forward_step(c, carry):
        s1, s2 = carry
        cs = pl.multiple_of(c * CH, CH)
        g = c // (inner_chunks // groups)
        stepx, ex, colb, rowb = chunk_tables(c)
        x = co[:, pl.ds(cs, CH)]
        xh, xl = split2(x * stepx)
        score = sc[g]
        w = jnp.concatenate(
            [
                jnp.exp(jnp.where(causal, colb[:, h * rows : (h + 1) * rows] - rowb[h], -1e30))
                * score
                for h in range(HC)
            ],
            axis=1,
        )
        wh, wl = split2(w)
        bh, bl = block_diag(xh), block_diag(xl)
        within = dot(wh, bh) + dot(wh, bl) + dot(wl, bh)
        carried = jnp.zeros((rows, CH), F32)
        for d in range(docs):
            state = state_of(d, c)
            carried = carried + dot(cmh[g, :, d * N : (d + 1) * N], state, NT)
            carried = carried + dot(cml[g, :, d * N : (d + 1) * N], state, NT)
        y = within + ex * carried + wv_ref[6:7, pl.ds(cs, CH)] * x
        ybuf[:, pl.ds(cs, CH)] = y
        z = recv_ref[0, :, pl.ds(zoff + cs, CH)].astype(F32)
        up = recv_ref[0, :, pl.ds(upoff + cs, CH)].astype(F32)
        v = y * (z * jax.nn.sigmoid(z))
        p1 = v * v
        p2 = up * wv_ref[5:6, pl.ds(cs, CH)] * v
        return s1 + p1[:, :128] + p1[:, 128:], s2 + p2[:, :128] + p2[:, 128:]

    zeros = jnp.zeros((rows, 128), F32)
    s1, s2 = lax.fori_loop(0, inner_chunks, forward_step, (zeros, zeros))
    inv = lax.rsqrt(jnp.sum(s1, axis=1, keepdims=True) / GS + 1e-05)
    mean2 = jnp.sum(s2, axis=1, keepdims=True) * wtok / GS
    coef = inv * inv * inv * mean2

    def backward_step(c, carry):
        cs = pl.multiple_of(c * CH, CH)
        g = c // (inner_chunks // groups)
        stepx, ex, colb, rowb = chunk_tables(c)
        x = co[:, pl.ds(cs, CH)]
        y = ybuf[:, pl.ds(cs, CH)]
        z = recv_ref[0, :, pl.ds(zoff + cs, CH)].astype(F32)
        up = recv_ref[0, :, pl.ds(upoff + cs, CH)].astype(F32)
        skip = wv_ref[6:7, pl.ds(cs, CH)]
        sg = jax.nn.sigmoid(z)
        sz = z * sg
        v = y * sz
        dn = up * (wtok * inv)
        wg_ref[5:6, pl.ds(cs, CH)] += colsum(dn * v)
        dv = dn * wv_ref[5:6, pl.ds(cs, CH)] - v * coef
        dy = dv * sz
        out_ref[0, :, pl.ds(chans + cs, CH)] = (dv * y * (sg * (1.0 + z * (1.0 - sg)))).astype(
            BF16
        )
        xs = x * stepx
        xh, xl = split2(xs)
        dyh, dyl = split2(dy)
        bh, bl = block_diag(xh), block_diag(xl)
        dm = dot(dyh, bh, NT) + dot(dyh, bl, NT) + dot(dyl, bh, NT)
        score_t = sct[g]
        total = dsc[g]
        wt = []
        for h in range(HC):
            gap = colb[:, h * rows : (h + 1) * rows] - rowb[h]
            total = total + jnp.exp(jnp.where(causal, gap, -1e30)) * dm[:, h * rows : (h + 1) * rows]
            wt.append(jnp.exp(jnp.where(causal_t, -gap, -1e30)) * score_t)
        dsc[g] = total
        wh, wl = split2(jnp.concatenate(wt, axis=1))
        dh, dl = block_diag(dyh), block_diag(dyl)
        dxs = dot(wh, dh) + dot(wh, dl) + dot(wl, dh)
        dco[:, pl.ds(cs, CH)] = stepx * dxs + skip * dy
        wg_ref[6:7, pl.ds(cs, CH)] += colsum(dy * x)
        both = jnp.concatenate([dy * (y - skip * x) - xs * dxs, dxs * x], axis=0)
        pick = jnp.where(
            lax.broadcasted_iota(jnp.int32, (CH, heads), 0) // P_SIZE + c * HC
            == lax.broadcasted_iota(jnp.int32, (CH, heads), 1),
            1.0,
            0.0,
        ).astype(BF16)
        b1, b2, b3 = split3(both)
        dred[...] += dot(b1, pick) + dot(b2, pick) + dot(b3, pick)
        q = ex * dy
        qh, ql = split2(q)
        qth, qtl = split2(q.T)
        ch, cl = cmh[g], cml[g]
        ds_all = dot(qth, ch) + dot(qtl, ch) + dot(qth, cl)
        back = jnp.zeros((rows, N), F32)
        for d in range(docs):
            p = prompt_ref[k * docs + d]
            acc[pl.ds(c * nf, nf), p] += ds_all[:, d * N : (d + 1) * N].reshape(nf, share_rows, N)
            state = state_of(d, c)
            back = back + jnp.where(doc_col == d, dot(qh, state) + dot(ql, state), 0.0)
        dcc[g] += back
        return carry

    lax.fori_loop(0, inner_chunks, backward_step, 0)

    @pl.when(k == pl.num_programs(0) - 1)
    def _():
        pltpu.make_async_copy(acc, dstate_ref, out_sem).start()

    for g in range(groups):
        bg = co[:, b_off + g * N : b_off + (g + 1) * N]
        cg = co[:, c_off + g * N : c_off + (g + 1) * N]
        dco[:, c_off + g * N : c_off + (g + 1) * N] = dot3(dsc[g], bg) + dcc[g]
        dco[:, b_off + g * N : b_off + (g + 1) * N] = dot3(dsc[g].T, cg)

    ddec = exact_left(jnp.where(causal_t, 1.0, 0.0).astype(BF16), dred[0:rows])
    ddt = (dred[rows : 2 * rows] + ddec * rate) * jax.nn.sigmoid(dt_pre)
    wg_ref[7:8, 0:heads] += colsum(ddt)
    wg_ref[8:9, 0:heads] += colsum(ddec * dec)
    out_ref[0, :, chans + inner :] = jnp.concatenate(
        list(split3(ddt)) + [jnp.zeros((rows, 128 - 3 * heads), BF16)], axis=1
    )

    def conv_back(i, carry):
        cs = pl.multiple_of(i * CH, CH)
        pre, taps, w = conv(cs)
        sg = jax.nn.sigmoid(pre)
        dpre = dco[:, pl.ds(cs, CH)] * (sg * (1.0 + pre * (1.0 - sg)))
        for j in range(4):
            wg_ref[3 - j : 4 - j, pl.ds(cs, CH)] += colsum(dpre * taps[j])
        wg_ref[4:5, pl.ds(cs, CH)] += colsum(dpre)
        hi, lo = split2(jnp.concatenate([w[j] * dpre for j in (1, 2, 3)], axis=0))
        du = dot(shift_t, hi) + dot(shift_t, lo)
        out_ref[0, :, pl.ds(cs, CH)] = (w[0] * dpre + du[0:rows]).astype(BF16)
        dtail_ref[0, :, pl.ds(cs, CH)] = du[rows : rows + 16]
        return carry

    lax.fori_loop(0, all_chunks, conv_back, 0)

    @pl.when(k == pl.num_programs(0) - 1)
    def _():
        pltpu.make_async_copy(acc, dstate_ref, out_sem).wait()


def run_mixer(prompts, adv, recv, tails, wv, hv, states, docs):
    blocks, rows, width = recv.shape
    chans = wv.shape[1]
    fcount, prompt_count, share_rows, _ = states.shape
    inner = fcount * share_rows
    heads = inner // P_SIZE
    groups = (chans - inner) // (2 * N)
    dims = (rows, docs, chans, inner, heads, groups, fcount, share_rows)
    out_width = chans + inner + 128
    smem = pl.BlockSpec(memory_space=pltpu.SMEM)
    hbm = pl.BlockSpec(memory_space=pl.ANY)
    return pl.pallas_call(
        functools.partial(mixer_kernel, dims),
        grid=(blocks,),
        in_specs=[
            smem,
            smem,
            pl.BlockSpec((1, rows, width), lambda i: (i, 0, 0)),
            pl.BlockSpec((1, 16, chans), lambda i: (i, 0, 0)),
            pl.BlockSpec(wv.shape, lambda i: (0, 0)),
            pl.BlockSpec(hv.shape, lambda i: (0, 0)),
            hbm,
        ],
        out_specs=[
            pl.BlockSpec((1, rows, out_width), lambda i: (i, 0, 0)),
            hbm,
            pl.BlockSpec((1, 16, chans), lambda i: (i, 0, 0)),
            pl.BlockSpec((16, chans), lambda i: (0, 0)),
        ],
        out_shape=[
            jax.ShapeDtypeStruct((blocks, rows, out_width), BF16),
            jax.ShapeDtypeStruct(states.shape, F32),
            jax.ShapeDtypeStruct((blocks, 16, chans), F32),
            jax.ShapeDtypeStruct((16, chans), F32),
        ],
        scratch_shapes=[
            pltpu.VMEM((docs, fcount, share_rows, N), BF16),
            pltpu.VMEM(states.shape, F32),
            pltpu.VMEM((2 * rows, chans), BF16),
            pltpu.VMEM((rows, chans), F32),
            pltpu.VMEM((rows, chans), F32),
            pltpu.VMEM((rows, inner), F32),
            pltpu.VMEM((groups, rows, rows), F32),
            pltpu.VMEM((groups, rows, rows), F32),
            pltpu.VMEM((groups, rows, docs * N), BF16),
            pltpu.VMEM((groups, rows, docs * N), BF16),
            pltpu.VMEM((heads, rows), F32),
            pltpu.VMEM((rows, 3 * heads), BF16),
            pltpu.VMEM((2 * rows, 3 * heads), BF16),
            pltpu.VMEM((2 * rows, heads), F32),
            pltpu.VMEM((groups, rows, rows), F32),
            pltpu.VMEM((groups, rows, N), F32),
            pltpu.SemaphoreType.DMA((docs,)),
            pltpu.SemaphoreType.DMA,
        ],
        compiler_params=pltpu.CompilerParams(
            dimension_semantics=("arbitrary",), vmem_limit_bytes=60 * 1024 * 1024
        ),
        cost_estimate=pl.CostEstimate(
            flops=20_000_000_000, bytes_accessed=30_000_000, transcendentals=10_000_000
        ),
        name="mixer",
    )(prompts, adv, recv, tails, wv, hv, states)


def pack_kernel(dims, me, xp, bp, cp, zp, upp, dtp, lenp, out):
    inner, gn, heads, docs = dims
    rows = xp.shape[0]
    i = me[0] ^ pl.program_id(0)
    at = 0
    for ref in (xp, bp, cp, zp, upp):
        width = ref.shape[1]
        out[0, :, at : at + width] = ref[...]
        at += width
    lane = lax.broadcasted_iota(jnp.int32, (1, dtp.shape[1]), 1) // heads
    own = jnp.where(lane == i, dtp[...], 0.0)
    dt = sum(own[:, j * heads : (j + 1) * heads] for j in range(dtp.shape[1] // heads))
    lens = jnp.broadcast_to(lenp[...].astype(F32), (rows, docs)).astype(BF16)
    pad = jnp.zeros((rows, 128 - 3 * heads - docs), BF16)
    out[0, :, at:] = jnp.concatenate(list(split3(dt)) + [lens, pad], axis=1)


def pack(me, xbc, zgate, upstream, dt_raw, resp_lengths, dp_count):
    rows = xbc.shape[0]
    docs = resp_lengths.shape[1]
    inner, gn, heads = DI // dp_count, GN // dp_count, H // dp_count
    width = 3 * inner + 2 * gn + 128
    return pl.pallas_call(
        functools.partial(pack_kernel, (inner, gn, heads, docs)),
        grid_spec=pltpu.PrefetchScalarGridSpec(
            num_scalar_prefetch=1,
            grid=(dp_count,),
            in_specs=[
                pl.BlockSpec((rows, inner), lambda o, me: (0, o ^ me[0])),
                pl.BlockSpec((rows, gn), lambda o, me: (0, DI // gn + (o ^ me[0]))),
                pl.BlockSpec((rows, gn), lambda o, me: (0, (DI + GN) // gn + (o ^ me[0]))),
                pl.BlockSpec((rows, inner), lambda o, me: (0, o ^ me[0])),
                pl.BlockSpec((rows, inner), lambda o, me: (0, o ^ me[0])),
                pl.BlockSpec(dt_raw.shape, lambda o, me: (0, 0)),
                pl.BlockSpec(resp_lengths.shape, lambda o, me: (0, 0)),
            ],
            out_specs=pl.BlockSpec((1, rows, width), lambda o, me: (o, 0, 0)),
        ),
        out_shape=jax.ShapeDtypeStruct((dp_count, rows, width), BF16),
        compiler_params=pltpu.CompilerParams(
            dimension_semantics=("arbitrary",), vmem_limit_bytes=32 * 1024 * 1024
        ),
        name="pack",
    )(me, xbc, xbc, xbc, zgate, upstream, dt_raw, resp_lengths)


def unpack_kernel(dims, me, back, gx, gz, gdt):
    inner, gn, heads = dims
    i = me[0] ^ pl.program_id(0)
    gx[:, pl.ds(pl.multiple_of(i * inner, inner), inner)] = back[0, :, 0:inner]
    gx[:, pl.ds(pl.multiple_of(DI + i * gn, gn), gn)] = back[0, :, inner : inner + gn]
    gx[:, pl.ds(pl.multiple_of(DI + GN + i * gn, gn), gn)] = back[
        0, :, inner + gn : inner + 2 * gn
    ]
    gz[...] = back[0, :, inner + 2 * gn : 2 * inner + 2 * gn]
    meta = back[0, :, 2 * inner + 2 * gn :].astype(F32)
    dt = meta[:, 0:heads] + meta[:, heads : 2 * heads] + meta[:, 2 * heads : 3 * heads]
    wide = jnp.concatenate([dt] * (H // heads), axis=1)
    lane = lax.broadcasted_iota(jnp.int32, (1, H), 1) // heads
    gdt[...] = jnp.where(lane == i, wide, gdt[...])


def unpack(me, back):
    dp_count, rows, width = back.shape
    inner, gn, heads = DI // dp_count, GN // dp_count, H // dp_count
    return pl.pallas_call(
        functools.partial(unpack_kernel, (inner, gn, heads)),
        grid_spec=pltpu.PrefetchScalarGridSpec(
            num_scalar_prefetch=1,
            grid=(dp_count,),
            in_specs=[pl.BlockSpec((1, rows, width), lambda o, me: (o, 0, 0))],
            out_specs=[
                pl.BlockSpec((rows, DI + 2 * GN), lambda o, me: (0, 0)),
                pl.BlockSpec((rows, inner), lambda o, me: (0, o ^ me[0])),
                pl.BlockSpec((rows, H), lambda o, me: (0, 0)),
            ],
        ),
        out_shape=[
            jax.ShapeDtypeStruct((rows, DI + 2 * GN), BF16),
            jax.ShapeDtypeStruct((rows, DI), BF16),
            jax.ShapeDtypeStruct((rows, H), F32),
        ],
        compiler_params=pltpu.CompilerParams(
            dimension_semantics=("arbitrary",), vmem_limit_bytes=32 * 1024 * 1024
        ),
        name="unpack",
    )(me, back)


def swap_blocks(blocks, count):
    got = [blocks[0]]
    for o in range(1, count):
        got.append(lax.ppermute(blocks[o], "dp", [(i, i ^ o) for i in range(count)]))
    return jnp.stack(got)


def ring_sums(table, at, count):
    ring = list(range(0, count, 2)) + list(range(1, count, 2))[::-1]
    place = [ring.index(j) for j in range(count)]
    ring_at = jnp.asarray(ring, jnp.int32)
    here = jnp.asarray(place, jnp.int32)[at]
    half = table.shape[1] // 2

    def part(way, steps):
        owner = ring_at[(here - way * (1 + steps)) % count]
        start = (owner, 0 if way == 1 else half, 0, 0)
        return lax.dynamic_slice(table, start, (1, half) + table.shape[2:])[0]

    held = {way: part(way, 0) for way in (1, -1)}
    for hop in range(1, count):
        for way in (1, -1):
            pairs = [(ring[r], ring[(r + way) % count]) for r in range(count)]
            held[way] = lax.ppermute(held[way], "fsdp", pairs) + part(way, hop)
    return jnp.concatenate([held[1], held[-1]], axis=0)


def to_all(a, axes, count):
    many = jnp.broadcast_to(a[None], (count,) + a.shape)
    return lax.all_to_all(many, axes, split_axis=0, concat_axis=0, tiled=True)


def shards(
    xbc,
    zgate,
    dt_raw,
    prompt_states,
    conv_tails,
    resp_prompt,
    resp_lengths,
    rewards,
    upstream,
    conv_weight,
    conv_bias,
    dt_bias,
    a_log,
    d_skip,
    norm_gain,
):
    dp_count = lax.axis_size("dp")
    fsdp_count = lax.axis_size("fsdp")
    dp_at = lax.axis_index("dp")
    fsdp_at = lax.axis_index("fsdp")
    docs = resp_lengths.shape[1]
    rows = xbc.shape[0]
    prompt_count, head_share = prompt_states.shape[:2]
    chan_share = conv_tails.shape[2]
    inner = DI // dp_count
    gn = GN // dp_count
    chans = inner + 2 * gn
    heads = H // dp_count

    me = dp_at.astype(jnp.int32).reshape(1)
    sent = pack(me, xbc, zgate, upstream, dt_raw, resp_lengths, dp_count)
    recv = swap_blocks(sent, dp_count)

    states = lax.all_gather(
        prompt_states.reshape(prompt_count, head_share * P_SIZE, N), "fsdp", axis=0
    )

    chan_w = conv_weight.shape[1]
    flat = jnp.concatenate(
        [conv_weight.reshape(-1), conv_bias, norm_gain, dt_bias, a_log, d_skip]
    )
    flat = to_all(flat, "fsdp", fsdp_count)
    conv_all = flat[:, : 5 * chan_w].reshape(fsdp_count, 5, chan_w).transpose(1, 0, 2)
    conv_all = conv_all.reshape(5, fsdp_count * chan_w)
    gain_w = norm_gain.shape[0]
    gain_all = flat[:, 5 * chan_w : 5 * chan_w + gain_w].reshape(-1)
    per_head = flat[:, 5 * chan_w + gain_w :].reshape(fsdp_count, 3, -1).transpose(1, 0, 2)
    per_head = lax.dynamic_slice_in_dim(per_head.reshape(3, H), dp_at * heads, heads, 1)

    def own_channels(a):
        return jnp.concatenate(
            [
                lax.dynamic_slice_in_dim(a, dp_at * inner, inner, a.ndim - 1),
                lax.dynamic_slice_in_dim(a, DI + dp_at * gn, gn, a.ndim - 1),
                lax.dynamic_slice_in_dim(a, DI + GN + dp_at * gn, gn, a.ndim - 1),
            ],
            axis=-1,
        )

    def pad_row(a):
        return jnp.pad(a, (0, chans - inner))[None]

    wv = jnp.concatenate(
        [
            own_channels(conv_all),
            pad_row(lax.dynamic_slice_in_dim(gain_all, dp_at * inner, inner)),
            pad_row(jnp.repeat(per_head[2], P_SIZE)),
            jnp.zeros((1, chans), F32),
        ]
    )
    hv = jnp.concatenate([per_head[:2], jnp.zeros((6, heads), F32)])

    holders = (jnp.arange(dp_count, dtype=jnp.int32) ^ dp_at) * fsdp_count + fsdp_at
    prompts = resp_prompt.reshape(-1, docs)[holders].reshape(-1)
    adv = advantages(rewards, resp_prompt, prompt_count)
    adv = adv.reshape(-1, docs)[holders].reshape(-1)

    tails = to_all(conv_tails, ("dp", "fsdp"), dp_count * fsdp_count)
    tails = tails.transpose(1, 2, 0, 3).reshape(prompt_count, 3, -1)
    tails = jnp.pad(own_channels(tails), ((0, 0), (0, 1), (0, 0)))
    tails = tails[prompts].reshape(dp_count, docs * 4, chans)

    out, dstate, dtail, wg = run_mixer(prompts, adv, recv, tails, wv, hv, states, docs)

    grad_states = ring_sums(dstate, fsdp_at, fsdp_count)
    grad_states = grad_states.reshape(prompt_count, head_share, P_SIZE, N)

    back = swap_blocks(out, dp_count)

    grad_x, grad_z, grad_dt = unpack(me, back)

    onehot = (jnp.arange(prompt_count, dtype=jnp.int32)[:, None] == prompts[None, :]).astype(F32)
    dtail = dtail.reshape(dp_count * docs, 4, chans)[:, :3].reshape(dp_count * docs, 3 * chans)
    dtail = jnp.dot(onehot, dtail, precision=lax.Precision.HIGHEST)

    def spread(a, lead):
        full = jnp.zeros((lead, DI + 2 * GN), F32)
        full = lax.dynamic_update_slice(full, a[:, :inner], (0, dp_at * inner))
        full = lax.dynamic_update_slice(full, a[:, inner : inner + gn], (0, DI + dp_at * gn))
        return lax.dynamic_update_slice(full, a[:, inner + gn :], (0, DI + GN + dp_at * gn))

    tail_full = spread(dtail.reshape(prompt_count * 3, chans), prompt_count * 3)
    tail_full = tail_full.reshape(prompt_count * 3, dp_count, fsdp_count, chan_share)
    tail_full = tail_full.transpose(2, 1, 0, 3).reshape(fsdp_count, -1)
    conv_full = spread(wg[:5], 5).reshape(5, fsdp_count, chan_w).transpose(1, 0, 2)
    gain_full = lax.dynamic_update_slice(jnp.zeros((DI,), F32), wg[5, :inner], (dp_at * inner,))
    skip_grad = jnp.sum(wg[6, :inner].reshape(heads, P_SIZE), axis=1)
    head_grad = jnp.stack([wg[7, :heads], wg[8, :heads], skip_grad])
    head_full = lax.dynamic_update_slice(jnp.zeros((3, H), F32), head_grad, (0, dp_at * heads))
    head_full = head_full.reshape(3, fsdp_count, -1).transpose(1, 0, 2)
    payload = jnp.concatenate(
        [
            tail_full,
            conv_full.reshape(fsdp_count, -1),
            gain_full.reshape(fsdp_count, -1),
            head_full.reshape(fsdp_count, -1),
        ],
        axis=1,
    )
    used = payload.shape[1]
    lines = -(-used // 1024) * 8
    payload = jnp.pad(payload, ((0, 0), (0, lines * 128 - used))).reshape(fsdp_count, lines, 128)
    summed = lax.psum_scatter(payload, "fsdp", scatter_dimension=0, tiled=False)
    summed = summed.reshape(-1)[:used]
    tail_size = prompt_count * 3 * chan_share
    shared = summed[dp_count * tail_size :]
    pieces = jnp.concatenate(
        [
            summed[: dp_count * tail_size].reshape(dp_count, tail_size),
            jnp.broadcast_to(shared[None], (dp_count,) + shared.shape),
        ],
        axis=1,
    )
    summed = jnp.sum(lax.all_to_all(pieces, "dp", split_axis=0, concat_axis=0, tiled=True), axis=0)
    grad_tails = summed[:tail_size].reshape(prompt_count, 3, chan_share)
    rest = summed[tail_size:]
    grad_conv = rest[: 5 * chan_w].reshape(5, chan_w)
    rest = rest[5 * chan_w :]
    per = dt_bias.shape[0]
    return (
        grad_x,
        grad_z,
        grad_dt,
        grad_states,
        grad_tails,
        grad_conv[:4],
        grad_conv[4],
        rest[gain_w : gain_w + per],
        rest[gain_w + per : gain_w + 2 * per],
        rest[gain_w + 2 * per : gain_w + 3 * per],
        rest[:gain_w],
    )


def solution(mesh):
    return jax.shard_map(
        shards,
        mesh=mesh,
        in_specs=(
            P(("dp", "fsdp"), None),
            P(("dp", "fsdp"), None),
            P(("dp", "fsdp"), None),
            P(None, ("dp", "fsdp"), None, None),
            P(None, None, ("dp", "fsdp")),
            P(),
            P(("dp", "fsdp"), None),
            P(),
            P(("dp", "fsdp"), None),
            P(None, "fsdp"),
            P("fsdp"),
            P("fsdp"),
            P("fsdp"),
            P("fsdp"),
            P("fsdp"),
        ),
        out_specs=(
            P(("dp", "fsdp"), None),
            P(("dp", "fsdp"), None),
            P(("dp", "fsdp"), None),
            P(None, ("dp", "fsdp"), None, None),
            P(None, None, ("dp", "fsdp")),
            P(None, "fsdp"),
            P("fsdp"),
            P("fsdp"),
            P("fsdp"),
            P("fsdp"),
            P("fsdp"),
        ),
        check_vma=False,
    )
```

```python
import functools

import jax
import jax.numpy as jnp
from jax import lax
from jax.experimental import pallas as pl
from jax.experimental.pallas import tpu as pltpu
from jax.sharding import PartitionSpec as P

GROUP = 16
H = 128
P_SIZE = 64
N = 128
G = 8
GS = 2048
DI = H * P_SIZE
GN = G * N

CH = 256
HC = CH // P_SIZE
F32 = jnp.float32
BF16 = jnp.bfloat16
NN = (((1,), (0,)), ((), ()))
NT = (((1,), (1,)), ((), ()))


def advantages(rewards, resp_prompt, prompt_count):
    member = (resp_prompt[:, None] == jnp.arange(prompt_count, dtype=jnp.int32)[None, :]).astype(
        jnp.float32
    )
    group_mean = jnp.dot(rewards, member, precision=lax.Precision.HIGHEST) / GROUP
    centred = rewards - jnp.dot(member, group_mean, precision=lax.Precision.HIGHEST)
    spread = jnp.sqrt(jnp.dot(centred * centred, member, precision=lax.Precision.HIGHEST) / GROUP)
    return centred / jnp.dot(member, jnp.maximum(spread, 0.8), precision=lax.Precision.HIGHEST)


def dot(a, b, dims=NN):
    return lax.dot_general(a, b, dims, preferred_element_type=F32)


def split2(a):
    hi = a.astype(BF16)
    return hi, (a - hi.astype(F32)).astype(BF16)


def split3(a):
    hi = a.astype(BF16)
    rest = a - hi.astype(F32)
    mid = rest.astype(BF16)
    return hi, mid, (rest - mid.astype(F32)).astype(BF16)


def dot3(a, b, dims=NN):
    ah, al = split2(a)
    bh, bl = split2(b)
    return dot(ah, bh, dims) + dot(ah, bl, dims) + dot(al, bh, dims)


def exact_left(mask, table):
    hi, mid, lo = split3(table)
    return dot(mask, hi) + dot(mask, mid) + dot(mask, lo)


def colsum(a):
    return jnp.sum(a, axis=0, keepdims=True)


def mixer_kernel(
    dims,
    prompt_ref,
    adv_ref,
    recv_ref,
    tails_ref,
    wv_ref,
    hv_ref,
    states_ref,
    out_ref,
    dstate_ref,
    dtail_ref,
    wg_ref,
    st,
    acc,
    uext,
    co,
    dco,
    ybuf,
    sc,
    sct,
    cmh,
    cml,
    relt,
    rel3,
    se3,
    dred,
    dsc,
    dcc,
    sems,
    out_sem,
):
    rows, docs, chans, inner, heads, groups, fcount, share_rows = dims
    nf = CH // share_rows
    k = pl.program_id(0)
    inner_chunks = inner // CH
    all_chunks = chans // CH
    zoff, upoff, moff = chans, chans + inner, chans + 2 * inner
    b_off, c_off = inner, inner + groups * N

    copies = [
        pltpu.make_async_copy(states_ref.at[:, prompt_ref[k * docs + d]], st.at[d], sems.at[d])
        for d in range(docs)
    ]
    for copy in copies:
        copy.start()

    @pl.when(k == 0)
    def _():
        wg_ref[...] = jnp.zeros_like(wg_ref)
        uext[...] = jnp.zeros_like(uext)

        def clear(f, carry):
            acc[f] = jnp.zeros(acc.shape[1:], F32)
            return carry

        lax.fori_loop(0, fcount, clear, 0)

    meta = recv_ref[0, :, moff : moff + 128].astype(F32)
    lens = [meta[0:1, 96 + d : 97 + d] for d in range(docs)]
    tcol = lax.broadcasted_iota(jnp.int32, (rows, 1), 0).astype(F32)
    trow = lax.broadcasted_iota(jnp.int32, (1, rows), 1).astype(F32)
    doc_col, doc_row = jnp.zeros_like(tcol), jnp.zeros_like(trow)
    start_col, start_row = jnp.zeros_like(tcol), jnp.zeros_like(trow)
    begin = jnp.zeros((1, 1), F32)
    for d in range(docs - 1):
        begin = begin + lens[d]
        doc_col = doc_col + jnp.where(tcol >= begin, 1.0, 0.0)
        doc_row = doc_row + jnp.where(trow >= begin, 1.0, 0.0)
        start_col = jnp.where(tcol >= begin, begin, start_col)
        start_row = jnp.where(trow >= begin, begin, start_row)
    off_col, off_row = tcol - start_col, trow - start_row
    wtok = jnp.zeros_like(tcol)
    for d in range(docs):
        wtok = wtok + jnp.where(
            doc_col == d, adv_ref[k * docs + d] * (rows / (docs * lens[d])), 0.0
        )
    same = doc_col == doc_row
    causal = same & (tcol >= trow)
    causal_t = same & (trow >= tcol)

    ext_row = lax.broadcasted_iota(jnp.int32, (1, 2 * rows), 1).astype(F32)
    ext_col = lax.broadcasted_iota(jnp.int32, (rows + 16, 1), 0).astype(F32)
    shift, shift_t = [], []
    for j in (1, 2, 3):
        src_col = jnp.where(off_col >= j, tcol - j, rows + doc_col * 4 + (3 - j) + off_col)
        src_row = jnp.where(off_row >= j, trow - j, rows + doc_row * 4 + (3 - j) + off_row)
        shift.append(jnp.where(src_col == ext_row, 1.0, 0.0).astype(BF16))
        shift_t.append(jnp.where(src_row == ext_col, 1.0, 0.0).astype(BF16))
    shift = jnp.concatenate(shift, axis=0)
    shift_t = jnp.concatenate(shift_t, axis=1)

    uext[0:rows, :] = recv_ref[0, :, 0:chans]
    uext[rows : rows + 16, :] = tails_ref[0]

    def conv(cs):
        u = uext[:, pl.ds(cs, CH)]
        lag = dot(shift, u)
        taps = [u[0:rows].astype(F32)] + [lag[i * rows : (i + 1) * rows] for i in range(3)]
        w = [wv_ref[3 - j : 4 - j, pl.ds(cs, CH)] for j in range(4)]
        pre = wv_ref[4:5, pl.ds(cs, CH)] + sum(w[j] * taps[j] for j in range(4))
        return pre, taps, w

    def conv_step(i, carry):
        cs = pl.multiple_of(i * CH, CH)
        pre, _, _ = conv(cs)
        co[:, pl.ds(cs, CH)] = pre * jax.nn.sigmoid(pre)
        return carry

    lax.fori_loop(0, all_chunks, conv_step, 0)

    for g in range(groups):
        bg = co[:, b_off + g * N : b_off + (g + 1) * N]
        cg = co[:, c_off + g * N : c_off + (g + 1) * N]
        sc[g] = dot3(cg, bg, NT)
        sct[g] = dot3(bg, cg, NT)
        hi, lo = split2(cg)
        zero = jnp.zeros_like(hi)
        for d in range(docs):
            cmh[g, :, d * N : (d + 1) * N] = jnp.where(doc_col == d, hi, zero)
            cml[g, :, d * N : (d + 1) * N] = jnp.where(doc_col == d, lo, zero)
        dsc[g] = jnp.zeros((rows, rows), F32)
        dcc[g] = jnp.zeros((rows, N), F32)
    dred[...] = jnp.zeros_like(dred)

    dt_pre = meta[:, 0:32] + meta[:, 32:64] + meta[:, 64:96] + hv_ref[0:1, :]
    tail_exp = jnp.exp(-jnp.abs(dt_pre))
    step = jnp.maximum(dt_pre, 0.0) + jnp.log1p(tail_exp)
    rate = -jnp.exp(hv_ref[1:2, :])
    dec = step * rate
    rel = exact_left(jnp.where(causal, 1.0, 0.0).astype(BF16), dec)
    relt[...] = rel.T
    rel3[...] = jnp.concatenate(split3(rel), axis=1)
    se3[0:rows, :] = jnp.concatenate(split3(step), axis=1)
    se3[rows : 2 * rows, :] = jnp.concatenate(split3(jnp.exp(rel)), axis=1)

    def head_onehot(c, width):
        r = lax.broadcasted_iota(jnp.int32, (3 * heads, HC * width), 0)
        r = jnp.where(r >= 2 * heads, r - 2 * heads, jnp.where(r >= heads, r - heads, r))
        lane = lax.broadcasted_iota(jnp.int32, (3 * heads, HC * width), 1)
        return jnp.where(r == c * HC + lane // width, 1.0, 0.0).astype(BF16)

    lane_head = lax.broadcasted_iota(jnp.int32, (1, CH), 1) // P_SIZE

    def block_diag(a):
        zero = jnp.zeros_like(a)
        return jnp.concatenate([jnp.where(lane_head == h, a, zero) for h in range(HC)], axis=0)

    def chunk_tables(c):
        expand = dot(se3[...], head_onehot(c, P_SIZE))
        colb = dot(rel3[...], head_onehot(c, rows))
        rowb = [relt[pl.ds(c * HC + h, 1), :] for h in range(HC)]
        return expand[0:rows], expand[rows : 2 * rows], colb, rowb

    def state_of(d, c):
        return st[d, pl.ds(c * nf, nf)].reshape(CH, N)

    for copy in copies:
        copy.wait()

    def forward_step(c, carry):
        s1, s2 = carry
        cs = pl.multiple_of(c * CH, CH)
        g = c // (inner_chunks // groups)
        stepx, ex, colb, rowb = chunk_tables(c)
        x = co[:, pl.ds(cs, CH)]
        xh, xl = split2(x * stepx)
        score = sc[g]
        w = jnp.concatenate(
            [
                jnp.exp(jnp.where(causal, colb[:, h * rows : (h + 1) * rows] - rowb[h], -1e30))
                * score
                for h in range(HC)
            ],
            axis=1,
        )
        wh, wl = split2(w)
        bh, bl = block_diag(xh), block_diag(xl)
        within = dot(wh, bh) + dot(wh, bl) + dot(wl, bh)
        carried = jnp.zeros((rows, CH), F32)
        for d in range(docs):
            state = state_of(d, c)
            carried = carried + dot(cmh[g, :, d * N : (d + 1) * N], state, NT)
            carried = carried + dot(cml[g, :, d * N : (d + 1) * N], state, NT)
        y = within + ex * carried + wv_ref[6:7, pl.ds(cs, CH)] * x
        ybuf[:, pl.ds(cs, CH)] = y
        z = recv_ref[0, :, pl.ds(zoff + cs, CH)].astype(F32)
        up = recv_ref[0, :, pl.ds(upoff + cs, CH)].astype(F32)
        v = y * (z * jax.nn.sigmoid(z))
        p1 = v * v
        p2 = up * wv_ref[5:6, pl.ds(cs, CH)] * v
        return s1 + p1[:, :128] + p1[:, 128:], s2 + p2[:, :128] + p2[:, 128:]

    zeros = jnp.zeros((rows, 128), F32)
    s1, s2 = lax.fori_loop(0, inner_chunks, forward_step, (zeros, zeros))
    inv = lax.rsqrt(jnp.sum(s1, axis=1, keepdims=True) / GS + 1e-05)
    mean2 = jnp.sum(s2, axis=1, keepdims=True) * wtok / GS
    coef = inv * inv * inv * mean2

    def backward_step(c, carry):
        cs = pl.multiple_of(c * CH, CH)
        g = c // (inner_chunks // groups)
        stepx, ex, colb, rowb = chunk_tables(c)
        x = co[:, pl.ds(cs, CH)]
        y = ybuf[:, pl.ds(cs, CH)]
        z = recv_ref[0, :, pl.ds(zoff + cs, CH)].astype(F32)
        up = recv_ref[0, :, pl.ds(upoff + cs, CH)].astype(F32)
        skip = wv_ref[6:7, pl.ds(cs, CH)]
        sg = jax.nn.sigmoid(z)
        sz = z * sg
        v = y * sz
        dn = up * (wtok * inv)
        wg_ref[5:6, pl.ds(cs, CH)] += colsum(dn * v)
        dv = dn * wv_ref[5:6, pl.ds(cs, CH)] - v * coef
        dy = dv * sz
        out_ref[0, :, pl.ds(chans + cs, CH)] = (dv * y * (sg * (1.0 + z * (1.0 - sg)))).astype(
            BF16
        )
        xs = x * stepx
        xh, xl = split2(xs)
        dyh, dyl = split2(dy)
        bh, bl = block_diag(xh), block_diag(xl)
        dm = dot(dyh, bh, NT) + dot(dyh, bl, NT) + dot(dyl, bh, NT)
        score_t = sct[g]
        total = dsc[g]
        wt = []
        for h in range(HC):
            gap = colb[:, h * rows : (h + 1) * rows] - rowb[h]
            total = total + jnp.exp(jnp.where(causal, gap, -1e30)) * dm[:, h * rows : (h + 1) * rows]
            wt.append(jnp.exp(jnp.where(causal_t, -gap, -1e30)) * score_t)
        dsc[g] = total
        wh, wl = split2(jnp.concatenate(wt, axis=1))
        dh, dl = block_diag(dyh), block_diag(dyl)
        dxs = dot(wh, dh) + dot(wh, dl) + dot(wl, dh)
        dco[:, pl.ds(cs, CH)] = stepx * dxs + skip * dy
        wg_ref[6:7, pl.ds(cs, CH)] += colsum(dy * x)
        both = jnp.concatenate([dy * (y - skip * x) - xs * dxs, dxs * x], axis=0)
        pick = jnp.where(
            lax.broadcasted_iota(jnp.int32, (CH, heads), 0) // P_SIZE + c * HC
            == lax.broadcasted_iota(jnp.int32, (CH, heads), 1),
            1.0,
            0.0,
        ).astype(BF16)
        b1, b2, b3 = split3(both)
        dred[...] += dot(b1, pick) + dot(b2, pick) + dot(b3, pick)
        q = ex * dy
        qh, ql = split2(q)
        qth, qtl = split2(q.T)
        ch, cl = cmh[g], cml[g]
        ds_all = dot(qth, ch) + dot(qtl, ch) + dot(qth, cl)
        back = jnp.zeros((rows, N), F32)
        for d in range(docs):
            p = prompt_ref[k * docs + d]
            acc[pl.ds(c * nf, nf), p] += ds_all[:, d * N : (d + 1) * N].reshape(nf, share_rows, N)
            state = state_of(d, c)
            back = back + jnp.where(doc_col == d, dot(qh, state) + dot(ql, state), 0.0)
        dcc[g] += back
        return carry

    lax.fori_loop(0, inner_chunks, backward_step, 0)

    @pl.when(k == pl.num_programs(0) - 1)
    def _():
        pltpu.make_async_copy(acc, dstate_ref, out_sem).start()

    for g in range(groups):
        bg = co[:, b_off + g * N : b_off + (g + 1) * N]
        cg = co[:, c_off + g * N : c_off + (g + 1) * N]
        dco[:, c_off + g * N : c_off + (g + 1) * N] = dot3(dsc[g], bg) + dcc[g]
        dco[:, b_off + g * N : b_off + (g + 1) * N] = dot3(dsc[g].T, cg)

    ddec = exact_left(jnp.where(causal_t, 1.0, 0.0).astype(BF16), dred[0:rows])
    ddt = (dred[rows : 2 * rows] + ddec * rate) * jax.nn.sigmoid(dt_pre)
    wg_ref[7:8, 0:heads] += colsum(ddt)
    wg_ref[8:9, 0:heads] += colsum(ddec * dec)
    out_ref[0, :, chans + inner :] = jnp.concatenate(
        list(split3(ddt)) + [jnp.zeros((rows, 128 - 3 * heads), BF16)], axis=1
    )

    def conv_back(i, carry):
        cs = pl.multiple_of(i * CH, CH)
        pre, taps, w = conv(cs)
        sg = jax.nn.sigmoid(pre)
        dpre = dco[:, pl.ds(cs, CH)] * (sg * (1.0 + pre * (1.0 - sg)))
        for j in range(4):
            wg_ref[3 - j : 4 - j, pl.ds(cs, CH)] += colsum(dpre * taps[j])
        wg_ref[4:5, pl.ds(cs, CH)] += colsum(dpre)
        hi, lo = split2(jnp.concatenate([w[j] * dpre for j in (1, 2, 3)], axis=0))
        du = dot(shift_t, hi) + dot(shift_t, lo)
        out_ref[0, :, pl.ds(cs, CH)] = (w[0] * dpre + du[0:rows]).astype(BF16)
        dtail_ref[0, :, pl.ds(cs, CH)] = du[rows : rows + 16]
        return carry

    lax.fori_loop(0, all_chunks, conv_back, 0)

    @pl.when(k == pl.num_programs(0) - 1)
    def _():
        pltpu.make_async_copy(acc, dstate_ref, out_sem).wait()


def run_mixer(prompts, adv, recv, tails, wv, hv, states, docs):
    blocks, rows, width = recv.shape
    chans = wv.shape[1]
    fcount, prompt_count, share_rows, _ = states.shape
    inner = fcount * share_rows
    heads = inner // P_SIZE
    groups = (chans - inner) // (2 * N)
    dims = (rows, docs, chans, inner, heads, groups, fcount, share_rows)
    out_width = chans + inner + 128
    smem = pl.BlockSpec(memory_space=pltpu.SMEM)
    hbm = pl.BlockSpec(memory_space=pl.ANY)
    return pl.pallas_call(
        functools.partial(mixer_kernel, dims),
        grid=(blocks,),
        in_specs=[
            smem,
            smem,
            pl.BlockSpec((1, rows, width), lambda i: (i, 0, 0)),
            pl.BlockSpec((1, 16, chans), lambda i: (i, 0, 0)),
            pl.BlockSpec(wv.shape, lambda i: (0, 0)),
            pl.BlockSpec(hv.shape, lambda i: (0, 0)),
            hbm,
        ],
        out_specs=[
            pl.BlockSpec((1, rows, out_width), lambda i: (i, 0, 0)),
            hbm,
            pl.BlockSpec((1, 16, chans), lambda i: (i, 0, 0)),
            pl.BlockSpec((16, chans), lambda i: (0, 0)),
        ],
        out_shape=[
            jax.ShapeDtypeStruct((blocks, rows, out_width), BF16),
            jax.ShapeDtypeStruct(states.shape, F32),
            jax.ShapeDtypeStruct((blocks, 16, chans), F32),
            jax.ShapeDtypeStruct((16, chans), F32),
        ],
        scratch_shapes=[
            pltpu.VMEM((docs, fcount, share_rows, N), BF16),
            pltpu.VMEM(states.shape, F32),
            pltpu.VMEM((2 * rows, chans), BF16),
            pltpu.VMEM((rows, chans), F32),
            pltpu.VMEM((rows, chans), F32),
            pltpu.VMEM((rows, inner), F32),
            pltpu.VMEM((groups, rows, rows), F32),
            pltpu.VMEM((groups, rows, rows), F32),
            pltpu.VMEM((groups, rows, docs * N), BF16),
            pltpu.VMEM((groups, rows, docs * N), BF16),
            pltpu.VMEM((heads, rows), F32),
            pltpu.VMEM((rows, 3 * heads), BF16),
            pltpu.VMEM((2 * rows, 3 * heads), BF16),
            pltpu.VMEM((2 * rows, heads), F32),
            pltpu.VMEM((groups, rows, rows), F32),
            pltpu.VMEM((groups, rows, N), F32),
            pltpu.SemaphoreType.DMA((docs,)),
            pltpu.SemaphoreType.DMA,
        ],
        compiler_params=pltpu.CompilerParams(
            dimension_semantics=("arbitrary",), vmem_limit_bytes=60 * 1024 * 1024
        ),
        cost_estimate=pl.CostEstimate(
            flops=20_000_000_000, bytes_accessed=30_000_000, transcendentals=10_000_000
        ),
        name="mixer",
    )(prompts, adv, recv, tails, wv, hv, states)


def pack_kernel(dims, me, xp, bp, cp, zp, upp, dtp, lenp, out):
    inner, gn, heads, docs = dims
    rows = xp.shape[0]
    i = me[0] ^ pl.program_id(0)
    at = 0
    for ref in (xp, bp, cp, zp, upp):
        width = ref.shape[1]
        out[0, :, at : at + width] = ref[...]
        at += width
    lane = lax.broadcasted_iota(jnp.int32, (1, dtp.shape[1]), 1) // heads
    own = jnp.where(lane == i, dtp[...], 0.0)
    dt = sum(own[:, j * heads : (j + 1) * heads] for j in range(dtp.shape[1] // heads))
    lens = jnp.broadcast_to(lenp[...].astype(F32), (rows, docs)).astype(BF16)
    pad = jnp.zeros((rows, 128 - 3 * heads - docs), BF16)
    out[0, :, at:] = jnp.concatenate(list(split3(dt)) + [lens, pad], axis=1)


def pack(me, xbc, zgate, upstream, dt_raw, resp_lengths, dp_count):
    rows = xbc.shape[0]
    docs = resp_lengths.shape[1]
    inner, gn, heads = DI // dp_count, GN // dp_count, H // dp_count
    width = 3 * inner + 2 * gn + 128
    return pl.pallas_call(
        functools.partial(pack_kernel, (inner, gn, heads, docs)),
        grid_spec=pltpu.PrefetchScalarGridSpec(
            num_scalar_prefetch=1,
            grid=(dp_count,),
            in_specs=[
                pl.BlockSpec((rows, inner), lambda o, me: (0, o ^ me[0])),
                pl.BlockSpec((rows, gn), lambda o, me: (0, DI // gn + (o ^ me[0]))),
                pl.BlockSpec((rows, gn), lambda o, me: (0, (DI + GN) // gn + (o ^ me[0]))),
                pl.BlockSpec((rows, inner), lambda o, me: (0, o ^ me[0])),
                pl.BlockSpec((rows, inner), lambda o, me: (0, o ^ me[0])),
                pl.BlockSpec(dt_raw.shape, lambda o, me: (0, 0)),
                pl.BlockSpec(resp_lengths.shape, lambda o, me: (0, 0)),
            ],
            out_specs=pl.BlockSpec((1, rows, width), lambda o, me: (o, 0, 0)),
        ),
        out_shape=jax.ShapeDtypeStruct((dp_count, rows, width), BF16),
        compiler_params=pltpu.CompilerParams(
            dimension_semantics=("arbitrary",), vmem_limit_bytes=32 * 1024 * 1024
        ),
        name="pack",
    )(me, xbc, xbc, xbc, zgate, upstream, dt_raw, resp_lengths)


def unpack_kernel(dims, me, back, gx, gz, gdt):
    inner, gn, heads = dims
    i = me[0] ^ pl.program_id(0)
    gx[:, pl.ds(pl.multiple_of(i * inner, inner), inner)] = back[0, :, 0:inner]
    gx[:, pl.ds(pl.multiple_of(DI + i * gn, gn), gn)] = back[0, :, inner : inner + gn]
    gx[:, pl.ds(pl.multiple_of(DI + GN + i * gn, gn), gn)] = back[
        0, :, inner + gn : inner + 2 * gn
    ]
    gz[...] = back[0, :, inner + 2 * gn : 2 * inner + 2 * gn]
    meta = back[0, :, 2 * inner + 2 * gn :].astype(F32)
    dt = meta[:, 0:heads] + meta[:, heads : 2 * heads] + meta[:, 2 * heads : 3 * heads]
    wide = jnp.concatenate([dt] * (H // heads), axis=1)
    lane = lax.broadcasted_iota(jnp.int32, (1, H), 1) // heads
    gdt[...] = jnp.where(lane == i, wide, gdt[...])


def unpack(me, back):
    dp_count, rows, width = back.shape
    inner, gn, heads = DI // dp_count, GN // dp_count, H // dp_count
    return pl.pallas_call(
        functools.partial(unpack_kernel, (inner, gn, heads)),
        grid_spec=pltpu.PrefetchScalarGridSpec(
            num_scalar_prefetch=1,
            grid=(dp_count,),
            in_specs=[pl.BlockSpec((1, rows, width), lambda o, me: (o, 0, 0))],
            out_specs=[
                pl.BlockSpec((rows, DI + 2 * GN), lambda o, me: (0, 0)),
                pl.BlockSpec((rows, inner), lambda o, me: (0, o ^ me[0])),
                pl.BlockSpec((rows, H), lambda o, me: (0, 0)),
            ],
        ),
        out_shape=[
            jax.ShapeDtypeStruct((rows, DI + 2 * GN), BF16),
            jax.ShapeDtypeStruct((rows, DI), BF16),
            jax.ShapeDtypeStruct((rows, H), F32),
        ],
        compiler_params=pltpu.CompilerParams(
            dimension_semantics=("arbitrary",), vmem_limit_bytes=32 * 1024 * 1024
        ),
        name="unpack",
    )(me, back)


def swap_blocks(blocks, count):
    got = [blocks[0]]
    for o in range(1, count):
        got.append(lax.ppermute(blocks[o], "dp", [(i, i ^ o) for i in range(count)]))
    return jnp.stack(got)


def ring_sums(table, at, count):
    ring = list(range(0, count, 2)) + list(range(1, count, 2))[::-1]
    place = [ring.index(j) for j in range(count)]
    ring_at = jnp.asarray(ring, jnp.int32)
    here = jnp.asarray(place, jnp.int32)[at]
    half = table.shape[1] // 2

    def part(way, steps):
        owner = ring_at[(here - way * (1 + steps)) % count]
        start = (owner, 0 if way == 1 else half, 0, 0)
        return lax.dynamic_slice(table, start, (1, half) + table.shape[2:])[0]

    held = {way: part(way, 0) for way in (1, -1)}
    for hop in range(1, count):
        for way in (1, -1):
            pairs = [(ring[r], ring[(r + way) % count]) for r in range(count)]
            held[way] = lax.ppermute(held[way], "fsdp", pairs) + part(way, hop)
    return jnp.concatenate([held[1], held[-1]], axis=0)


def to_all(a, axes, count):
    many = jnp.broadcast_to(a[None], (count,) + a.shape)
    return lax.all_to_all(many, axes, split_axis=0, concat_axis=0, tiled=True)


def shards(
    xbc,
    zgate,
    dt_raw,
    prompt_states,
    conv_tails,
    resp_prompt,
    resp_lengths,
    rewards,
    upstream,
    conv_weight,
    conv_bias,
    dt_bias,
    a_log,
    d_skip,
    norm_gain,
):
    dp_count = lax.axis_size("dp")
    fsdp_count = lax.axis_size("fsdp")
    dp_at = lax.axis_index("dp")
    fsdp_at = lax.axis_index("fsdp")
    docs = resp_lengths.shape[1]
    rows = xbc.shape[0]
    prompt_count, head_share = prompt_states.shape[:2]
    chan_share = conv_tails.shape[2]
    inner = DI // dp_count
    gn = GN // dp_count
    chans = inner + 2 * gn
    heads = H // dp_count

    me = dp_at.astype(jnp.int32).reshape(1)
    sent = pack(me, xbc, zgate, upstream, dt_raw, resp_lengths, dp_count)
    recv = swap_blocks(sent, dp_count)

    states = lax.all_gather(
        prompt_states.reshape(prompt_count, head_share * P_SIZE, N), "fsdp", axis=0
    )

    chan_w = conv_weight.shape[1]
    flat = jnp.concatenate(
        [conv_weight.reshape(-1), conv_bias, norm_gain, dt_bias, a_log, d_skip]
    )
    flat = to_all(flat, "fsdp", fsdp_count)
    conv_all = flat[:, : 5 * chan_w].reshape(fsdp_count, 5, chan_w).transpose(1, 0, 2)
    conv_all = conv_all.reshape(5, fsdp_count * chan_w)
    gain_w = norm_gain.shape[0]
    gain_all = flat[:, 5 * chan_w : 5 * chan_w + gain_w].reshape(-1)
    per_head = flat[:, 5 * chan_w + gain_w :].reshape(fsdp_count, 3, -1).transpose(1, 0, 2)
    per_head = lax.dynamic_slice_in_dim(per_head.reshape(3, H), dp_at * heads, heads, 1)

    def own_channels(a):
        return jnp.concatenate(
            [
                lax.dynamic_slice_in_dim(a, dp_at * inner, inner, a.ndim - 1),
                lax.dynamic_slice_in_dim(a, DI + dp_at * gn, gn, a.ndim - 1),
                lax.dynamic_slice_in_dim(a, DI + GN + dp_at * gn, gn, a.ndim - 1),
            ],
            axis=-1,
        )

    def pad_row(a):
        return jnp.pad(a, (0, chans - inner))[None]

    wv = jnp.concatenate(
        [
            own_channels(conv_all),
            pad_row(lax.dynamic_slice_in_dim(gain_all, dp_at * inner, inner)),
            pad_row(jnp.repeat(per_head[2], P_SIZE)),
            jnp.zeros((1, chans), F32),
        ]
    )
    hv = jnp.concatenate([per_head[:2], jnp.zeros((6, heads), F32)])

    holders = (jnp.arange(dp_count, dtype=jnp.int32) ^ dp_at) * fsdp_count + fsdp_at
    prompts = resp_prompt.reshape(-1, docs)[holders].reshape(-1)
    adv = advantages(rewards, resp_prompt, prompt_count)
    adv = adv.reshape(-1, docs)[holders].reshape(-1)

    tails = to_all(conv_tails, ("dp", "fsdp"), dp_count * fsdp_count)
    tails = tails.transpose(1, 2, 0, 3).reshape(prompt_count, 3, -1)
    tails = jnp.pad(own_channels(tails), ((0, 0), (0, 1), (0, 0)))
    tails = tails[prompts].reshape(dp_count, docs * 4, chans)

    out, dstate, dtail, wg = run_mixer(prompts, adv, recv, tails, wv, hv, states, docs)

    grad_states = ring_sums(dstate, fsdp_at, fsdp_count)
    grad_states = grad_states.reshape(prompt_count, head_share, P_SIZE, N)

    back = swap_blocks(out, dp_count)

    grad_x, grad_z, grad_dt = unpack(me, back)

    onehot = (jnp.arange(prompt_count, dtype=jnp.int32)[:, None] == prompts[None, :]).astype(F32)
    dtail = dtail.reshape(dp_count * docs, 4, chans)[:, :3].reshape(dp_count * docs, 3 * chans)
    dtail = jnp.dot(onehot, dtail, precision=lax.Precision.HIGHEST)

    def spread(a, lead):
        full = jnp.zeros((lead, DI + 2 * GN), F32)
        full = lax.dynamic_update_slice(full, a[:, :inner], (0, dp_at * inner))
        full = lax.dynamic_update_slice(full, a[:, inner : inner + gn], (0, DI + dp_at * gn))
        return lax.dynamic_update_slice(full, a[:, inner + gn :], (0, DI + GN + dp_at * gn))

    tail_full = spread(dtail.reshape(prompt_count * 3, chans), prompt_count * 3)
    tail_full = tail_full.reshape(prompt_count * 3, dp_count, fsdp_count, chan_share)
    tail_full = tail_full.transpose(2, 1, 0, 3).reshape(fsdp_count, -1)
    conv_full = spread(wg[:5], 5).reshape(5, fsdp_count, chan_w).transpose(1, 0, 2)
    gain_full = lax.dynamic_update_slice(jnp.zeros((DI,), F32), wg[5, :inner], (dp_at * inner,))
    skip_grad = jnp.sum(wg[6, :inner].reshape(heads, P_SIZE), axis=1)
    head_grad = jnp.stack([wg[7, :heads], wg[8, :heads], skip_grad])
    head_full = lax.dynamic_update_slice(jnp.zeros((3, H), F32), head_grad, (0, dp_at * heads))
    head_full = head_full.reshape(3, fsdp_count, -1).transpose(1, 0, 2)
    payload = jnp.concatenate(
        [
            tail_full,
            conv_full.reshape(fsdp_count, -1),
            gain_full.reshape(fsdp_count, -1),
            head_full.reshape(fsdp_count, -1),
        ],
        axis=1,
    )
    used = payload.shape[1]
    lines = -(-used // 1024) * 8
    payload = jnp.pad(payload, ((0, 0), (0, lines * 128 - used))).reshape(fsdp_count, lines, 128)
    summed = lax.psum_scatter(payload, "fsdp", scatter_dimension=0, tiled=False)
    summed = summed.reshape(-1)[:used]
    summed = jnp.where(dp_at < 0, grad_states[0, 0, 0, 0], summed)
    tail_size = prompt_count * 3 * chan_share
    shared = summed[dp_count * tail_size :]
    pieces = jnp.concatenate(
        [
            summed[: dp_count * tail_size].reshape(dp_count, tail_size),
            jnp.broadcast_to(shared[None], (dp_count,) + shared.shape),
        ],
        axis=1,
    )
    summed = jnp.sum(lax.all_to_all(pieces, "dp", split_axis=0, concat_axis=0, tiled=True), axis=0)
    grad_tails = summed[:tail_size].reshape(prompt_count, 3, chan_share)
    rest = summed[tail_size:]
    grad_conv = rest[: 5 * chan_w].reshape(5, chan_w)
    rest = rest[5 * chan_w :]
    per = dt_bias.shape[0]
    return (
        grad_x,
        grad_z,
        grad_dt,
        grad_states,
        grad_tails,
        grad_conv[:4],
        grad_conv[4],
        rest[gain_w : gain_w + per],
        rest[gain_w + per : gain_w + 2 * per],
        rest[gain_w + 2 * per : gain_w + 3 * per],
        rest[:gain_w],
    )


def solution(mesh):
    return jax.shard_map(
        shards,
        mesh=mesh,
        in_specs=(
            P(("dp", "fsdp"), None),
            P(("dp", "fsdp"), None),
            P(("dp", "fsdp"), None),
            P(None, ("dp", "fsdp"), None, None),
            P(None, None, ("dp", "fsdp")),
            P(),
            P(("dp", "fsdp"), None),
            P(),
            P(("dp", "fsdp"), None),
            P(None, "fsdp"),
            P("fsdp"),
            P("fsdp"),
            P("fsdp"),
            P("fsdp"),
            P("fsdp"),
        ),
        out_specs=(
            P(("dp", "fsdp"), None),
            P(("dp", "fsdp"), None),
            P(("dp", "fsdp"), None),
            P(None, ("dp", "fsdp"), None, None),
            P(None, None, ("dp", "fsdp")),
            P(None, "fsdp"),
            P("fsdp"),
            P("fsdp"),
            P("fsdp"),
            P("fsdp"),
            P("fsdp"),
        ),
        check_vma=False,
    )
```
